512 devices in a mesh: rep: 32 (over y_hi, z), fsdp: 16 (over y_lo, x, core).
Axes of the slice: x: 4, y: 4 (y_hi: 2, y_lo: 2; y = y_hi * 2 + y_lo), z: 16, core: 2. Of those that a mesh axis runs over, the one named last changes fastest.
Arguments:
- hidden: bfloat16 [512, 128, 5120], P(('rep', 'fsdp')), may hold values from -6 to 6
- norm_gain: float32 [5120], replicated, may hold values from 0.1 to 1.9
- quant_ref: bfloat16 [5120, 512], P('fsdp'), may hold values from -6 to 6
- scale_ref: float32 [4, 5120], P(None, 'fsdp'), may hold values from 0.007 to 0.028
- weight_prm: bfloat16 [5120, 512], P('fsdp'), may hold values from -0.078125 to 0.078125
- readout: bfloat16 [512, 128, 512], P(('rep', 'fsdp')), may hold values from -0.59765625 to 0.59765625
- lengths: int32 [512], P(('rep', 'fsdp')), may hold values from 32 to 128
- bounds: int32 [512, 8], P(('rep', 'fsdp')), may hold values from 0 to 127, as said below
- labels: int32 [512], P(('rep', 'fsdp')), may hold values from 0 to 1
Outputs:
- step_rewards: float32 [512, 8], P(('rep', 'fsdp'))
- grad_prm: float32 [5120, 512], P('fsdp')
The draws below stay inside these ranges and needn't reach their ends.
Inputs may be any that keep to these rules, and one draw needn't show every extreme that they name: bounds[s, 0] is 0 and bounds[s, j] lies in [j * 16, (j + 1) * 16).
All inputs are finite; a program needn't handle non-finite values.
Results may differ from the reference program's by a relative error of at most 0.0051.
Values may be sent and summed in bfloat16 or wider, within the bound.
No kernel may reach another device: no remote copies, remote signals or barrier semaphores. Data moves between devices by JAX's collectives and lax.ppermute only.
A program may use at most 64 MiB of HBM per device.

```python
import math
import jax
import jax.numpy as jnp
from jax import lax

D = 5120
HEAD = 128
HEADS = 4
LEN = 128
STEPS = 8
K = 512
SEQS = 512


def draw_lengths(key, part):
    key = jax.random.fold_in(key, 11)
    drawn = jax.random.randint(key, (SEQS,), LEN // 4, LEN + 1).astype(jnp.int32)
    drawn = drawn.at[0].set(LEN)
    return drawn.at[1].set(LEN // 4)


def draw_bounds(key, part):
    key = jax.random.fold_in(key, 23)
    stride = LEN // STEPS
    base = jnp.arange(STEPS, dtype=jnp.int32) * stride
    offset = jax.random.randint(key, (SEQS, STEPS), 0, stride).astype(jnp.int32)
    offset = offset.at[:, 0].set(0)
    offset = offset.at[0, STEPS - 1].set(stride - 1)
    return base[None, :] + offset


def place_ends(values, rng, smallest, high):
    longest = values.shape.index(max(values.shape))
    spots = []
    for shift in (0, 1):
        where = [jax.random.randint(jax.random.fold_in(rng, axis), (), 0, length) for axis, length in enumerate(values.shape)]
        where[longest] = (where[longest] + shift) % values.shape[longest]
        spots.append(tuple(where))
    return values.at[spots[0]].set(smallest).at[spots[1]].set(high)


def levels(key, dims, split, smallest, high):
    gain = 1.0
    for dim, blocks in split:
        draws = jax.random.uniform(jax.random.fold_in(jax.random.fold_in(key, 6), dim), (blocks,), jnp.float32, smallest / len(split), high / len(split))
        gain = gain * jnp.repeat(jnp.exp(draws), dims[dim] // blocks).reshape((-1,) + (1,) * (len(dims) - 1 - dim))
    return gain


def normal_values(own_key, extent, scale, reach, shards=(), kind=jnp.bfloat16):
    values = scale * jax.random.normal(own_key, extent, jnp.float32)
    if shards:
        values = values * levels(own_key, extent, shards, -0.22, 0.18)
    return jnp.clip(values, -reach, reach).astype(kind)


def setup_inputs(seed: int = 0) -> dict:
    arg_keys = jax.random.split(jax.random.key(seed), 10)
    hidden = normal_values(arg_keys[0], (SEQS, LEN, D), 1.0, 6.0, ((0, 512),))
    norm_gain = jnp.clip(1.0 + 0.18 * jax.random.normal(arg_keys[1], (D,), jnp.float32), 0.1, 1.9)
    quant_ref = normal_values(arg_keys[2], (D, K), 1.0, 6.0, ((0, 16),))
    scale_ref = jnp.clip(jnp.exp(math.log(0.028) - 1.3862944 * jax.random.uniform(arg_keys[3], (HEADS, D), jnp.float32) ** levels(arg_keys[3], (HEADS, D), ((1, 16),), -0.2, 0.2)), 0.007, 0.028)
    weight_prm = normal_values(arg_keys[4], (D, K), D ** -0.5, 0.078125, ((0, 16),))
    readout = normal_values(arg_keys[5], (SEQS, LEN, K), 0.1, 0.59765625, ((0, 512),))
    lengths = draw_lengths(jax.random.fold_in(arg_keys[9], 71), 0)
    bounds = draw_bounds(jax.random.fold_in(arg_keys[9], 71), 0)
    labels = place_ends(jax.random.randint(arg_keys[8], (SEQS,), 0, 2), jax.random.fold_in(arg_keys[8], 1), 0, 1).astype(jnp.int32)
    return {"hidden": hidden, "norm_gain": norm_gain, "quant_ref": quant_ref, "scale_ref": scale_ref, "weight_prm": weight_prm, "readout": readout, "lengths": lengths, "bounds": bounds, "labels": labels}


epsilon = 1e-06
beta_scale = 0.05

def reference(hidden, norm_gain, quant_ref, scale_ref, weight_prm, readout, lengths, bounds, labels):
    wide = hidden.astype(jnp.float32)
    mean_square = lax.optimization_barrier(jnp.mean(wide * wide, axis=-1, keepdims=True))
    normed = (wide * lax.rsqrt(mean_square + epsilon) * norm_gain).astype(jnp.bfloat16)
    expanded = jnp.repeat(scale_ref.T, HEAD, axis=1)
    ref_matrix = (quant_ref.astype(jnp.float32) * expanded).astype(jnp.bfloat16)
    flat_rows = normed.reshape(SEQS * LEN, D)
    value_prm = jnp.dot(flat_rows, weight_prm, preferred_element_type=jnp.float32)
    value_ref = jnp.dot(flat_rows, ref_matrix, preferred_element_type=jnp.float32)
    read_wide = readout.astype(jnp.float32).reshape(SEQS * LEN, K)
    margin = lax.optimization_barrier(jnp.sum((value_prm - value_ref) * read_wide, axis=-1)).reshape(SEQS, LEN)
    position = jnp.arange(LEN, dtype=jnp.int32)
    live = (position[None, :] < lengths[:, None]).astype(jnp.float32)
    reward = beta_scale * margin * live
    step_index = lax.optimization_barrier(jnp.sum((position[None, :, None] >= bounds[:, None, :]).astype(jnp.int32), axis=-1)) - 1
    onehot = (step_index[:, :, None] == jnp.arange(STEPS, dtype=jnp.int32)[None, None, :]).astype(jnp.float32)
    step_rewards = lax.optimization_barrier(jnp.sum(reward[:, :, None] * onehot, axis=1))
    total = lax.optimization_barrier(jnp.sum(reward, axis=1))
    weight_seq = beta_scale * (jax.nn.sigmoid(total) - labels.astype(jnp.float32))
    slope = (weight_seq[:, None, None] * live[:, :, None] * readout.astype(jnp.float32)).astype(jnp.bfloat16)
    slope_rows = slope.reshape(SEQS * LEN, K)
    grad_prm = lax.dot_general(flat_rows, slope_rows, (((0,), (0,)), ((), ())), preferred_element_type=jnp.float32)
    return (step_rewards, grad_prm)
```

```python
import jax
import jax.numpy as jnp
from jax import lax
from jax.sharding import Mesh, PartitionSpec as P

epsilon = 1e-06
beta_scale = 0.05

AXES = ("yh", "zh", "zl", "yl", "x", "c")
REP = ("yh", "zh", "zl")
FSDP = ("yl", "x", "c")
GROUP = ("x", "c")


def exchange(pieces, axes):
    return lax.all_to_all(pieces, axes, 0, 0, tiled=False)


def spread(block, axes):
    count = lax.axis_size(axes)
    return exchange(jnp.broadcast_to(block[None], (count,) + block.shape), axes)


def on_device(
    hidden, norm_gain, quant_ref, scale_ref, weight_prm, readout, lengths, bounds, labels
):
    seq_len, width = hidden.shape[1:]
    features = readout.shape[2]
    head_size = features // scale_ref.shape[0]
    steps_count = bounds.shape[1]
    rows = quant_ref.shape[0]
    group = lax.axis_size(GROUP)
    f32, bf16 = jnp.float32, jnp.bfloat16
    expanded = jnp.repeat(scale_ref.T, head_size, axis=1)
    ref_local = (quant_ref.astype(f32) * expanded).astype(bf16)
    delta = (weight_prm.astype(f32) - ref_local.astype(f32)).astype(bf16)
    delta_other = lax.ppermute(delta, "yl", [(0, 1), (1, 0)])
    y_lo = lax.axis_index("yl")
    delta_pair = jnp.where(
        y_lo == 0,
        jnp.concatenate([delta, delta_other], axis=0),
        jnp.concatenate([delta_other, delta], axis=0),
    )
    position = jnp.arange(seq_len, dtype=jnp.int32)
    live = position < lengths[0]
    masked = jnp.where(live[:, None], readout[0], jnp.zeros((), bf16))
    masked_group = lax.all_gather(masked, GROUP).reshape(group * seq_len, features)
    wide = hidden[0].astype(f32)
    mean_square = jnp.mean(wide * wide, axis=-1, keepdims=True)
    normed = (wide * lax.rsqrt(mean_square + epsilon) * norm_gain).astype(bf16)
    pieces = normed.reshape(seq_len, 2, group, rows).transpose(2, 0, 1, 3)
    columns = exchange(pieces.reshape(group, seq_len, 2 * rows), GROUP)
    columns = columns.reshape(group * seq_len, 2 * rows)
    value = jnp.dot(columns, delta_pair, preferred_element_type=f32)
    partial = jnp.sum(value * masked_group.astype(f32), axis=-1).reshape(group, seq_len)
    me = lax.axis_index(GROUP)
    own = (jnp.arange(group) == me).astype(f32) * labels[0].astype(f32)
    tags = jnp.pad(own[None, :], ((0, 7), (0, seq_len - group)))
    small = jnp.concatenate([partial, tags], axis=0)
    small = jnp.sum(spread(small, GROUP), axis=0)
    margin = small[:group]
    label_group = small[group, :group]
    total = jnp.sum(beta_scale * margin, axis=1)
    weight_seq = beta_scale * (jax.nn.sigmoid(total) - label_group)
    reward = beta_scale * lax.dynamic_slice_in_dim(margin, me, 1, axis=0)
    step_index = jnp.sum((position[:, None] >= bounds[0][None, :]).astype(jnp.int32), axis=-1) - 1
    onehot = (step_index[:, None] == jnp.arange(steps_count)[None, :]).astype(f32)
    step_rewards = jnp.sum(reward[0][:, None] * onehot, axis=0)[None]
    slope = (
        weight_seq[:, None, None] * masked_group.reshape(group, seq_len, features).astype(f32)
    ).astype(bf16)
    grad = lax.dot_general(
        columns,
        slope.reshape(group * seq_len, features),
        (((0,), (0,)), ((), ())),
        preferred_element_type=f32,
    )
    yh, zl = lax.axis_size("yh"), lax.axis_size("zl")
    part = rows // (yh * zl)
    grad = grad.astype(bf16).reshape(2, yh, zl, part, features).transpose(1, 0, 2, 3, 4)
    grad = exchange(grad.reshape(2 * yh * zl, part, features), ("yh", "yl", "zl"))
    grad = jnp.sum(grad.astype(f32), axis=0).astype(bf16)
    grad = jnp.sum(spread(grad, ("zh",)).astype(f32), axis=0).astype(bf16)
    grad = spread(grad, ("yh", "zl"))
    return step_rewards, grad.reshape(rows, features).astype(f32)


def solution(mesh):
    fine = Mesh(mesh.devices.reshape(2, 4, 4, 2, 4, 2), AXES)
    every = REP + FSDP
    in_specs = (
        P(every, None, None),
        P(),
        P(FSDP, None),
        P(None, FSDP),
        P(FSDP, None),
        P(every, None, None),
        P(every),
        P(every, None),
        P(every),
    )
    out_specs = (P(every, None), P(FSDP, None))
    return jax.shard_map(
        on_device, mesh=fine, in_specs=in_specs, out_specs=out_specs, check_vma=False
    )
```

```python
import jax
import jax.numpy as jnp
from jax import lax
from jax.experimental import pallas as pl
from jax.experimental.pallas import tpu as pltpu
from jax.sharding import Mesh, PartitionSpec as P

epsilon = 1e-06
beta_scale = 0.05

AXES = ("yh", "zh", "zl", "yl", "x", "c")
REP = ("yh", "zh", "zl")
FSDP = ("yl", "x", "c")
GROUP = ("x", "c")
VMEM_LIMIT = 24 * 1024 * 1024
VMEM = pl.BlockSpec(memory_space=pltpu.VMEM)
SMEM = pl.BlockSpec(memory_space=pltpu.SMEM)
f32, bf16 = jnp.float32, jnp.bfloat16


def exchange(pieces, axes):
    return lax.all_to_all(pieces, axes, 0, 0, tiled=False)


def spread(block, axes):
    count = lax.axis_size(axes)
    return exchange(jnp.broadcast_to(block[None], (count,) + block.shape), axes)


def wide_sum(parts):
    total = parts[0].astype(f32)
    for k in range(1, parts.shape[0]):
        total = total + parts[k].astype(f32)
    return total


def mask_kernel(lengths_ref, readout_ref, out_ref):
    position = lax.broadcasted_iota(jnp.int32, readout_ref.shape, 0)
    read = readout_ref[...].astype(f32)
    masked = jnp.where(position < lengths_ref[0], read, 0.0).astype(bf16)
    for k in range(out_ref.shape[0]):
        out_ref[k] = masked


def mask_call(lengths, readout, copies):
    return pl.pallas_call(
        mask_kernel,
        in_specs=[SMEM, VMEM],
        out_specs=VMEM,
        out_shape=jax.ShapeDtypeStruct((copies,) + readout.shape, bf16),
        compiler_params=pltpu.CompilerParams(vmem_limit_bytes=60 * 1024 * 1024),
    )(lengths, readout)


def norm_kernel(hidden_ref, gain_ref, pieces_ref):
    width = hidden_ref.shape[1]
    groups, _, two_rows = pieces_ref.shape
    rows = two_rows // 2
    wide = hidden_ref[...].astype(f32)
    mean_square = jnp.sum(wide * wide, axis=-1, keepdims=True) * (1.0 / width)
    scale = lax.rsqrt(mean_square + epsilon)
    normed = (wide * scale * gain_ref[...]).astype(bf16)
    for g in range(groups):
        low = normed[:, rows * g : rows * (g + 1)]
        high = normed[:, rows * (groups + g) : rows * (groups + g + 1)]
        pieces_ref[g] = jnp.concatenate([low, high], axis=1)


def norm_call(hidden, gain, groups):
    seq_len, width = hidden.shape
    share = width // groups
    block = 32
    return pl.pallas_call(
        norm_kernel,
        grid=(seq_len // block,),
        in_specs=[
            pl.BlockSpec((block, width), lambda i: (i, 0)),
            pl.BlockSpec((1, width), lambda i: (0, 0)),
        ],
        out_specs=pl.BlockSpec((groups, block, share), lambda i: (0, i, 0)),
        out_shape=jax.ShapeDtypeStruct((groups, seq_len, share), bf16),
        cost_estimate=pl.CostEstimate(
            flops=6 * seq_len * width, bytes_accessed=8 * seq_len * width, transcendentals=0
        ),
        compiler_params=pltpu.CompilerParams(vmem_limit_bytes=VMEM_LIMIT),
    )(hidden, gain)


def place_kernel(pieces_ref, out_ref):
    for k in range(pieces_ref.shape[0]):
        out_ref[:, 128 * k : 128 * (k + 1)] = pieces_ref[k].astype(f32)


def place_call(pieces, halves):
    count, part, lanes = pieces.shape
    across = count // halves
    return pl.pallas_call(
        place_kernel,
        grid=(halves,),
        in_specs=[pl.BlockSpec((across, part, lanes), lambda i: (i, 0, 0))],
        out_specs=pl.BlockSpec((part, across * lanes), lambda i: (i, 0)),
        out_shape=jax.ShapeDtypeStruct((halves * part, across * lanes), f32),
        compiler_params=pltpu.CompilerParams(vmem_limit_bytes=VMEM_LIMIT),
    )(pieces)


def seq_of(place_ref, j, swapped):
    core = place_ref[1]
    return 2 * j + (1 - core if swapped else core)


def margin_kernel(place_ref, tags_ref, columns_ref, own_ref, other_ref, near_ref, far_ref, out_ref):
    core, y_lo = place_ref[1], place_ref[2]
    me = 2 * place_ref[0] + core
    own, other = own_ref[...], other_ref[...]
    first = y_lo == 0
    delta = jnp.concatenate([jnp.where(first, own, other), jnp.where(first, other, own)], axis=0)
    groups, seq_len, _ = columns_ref.shape
    row = lax.broadcasted_iota(jnp.int32, (groups, seq_len), 0)
    acc = jnp.zeros((groups, seq_len), f32)
    for swapped, read_ref in ((False, near_ref), (True, far_ref)):
        for j in range(4):
            seq = seq_of(place_ref, j, swapped)
            value = jnp.dot(columns_ref[seq], delta, preferred_element_type=f32)
            prod = value * read_ref[j].astype(f32)
            lanes = prod.shape[1] // 128
            part = prod[:, :128]
            for k in range(1, lanes):
                part = part + prod[:, 128 * k : 128 * (k + 1)]
            line = jnp.sum(part.T, axis=0, keepdims=True)
            acc = jnp.where(row == seq, line, acc)
    label = tags_ref[0].astype(f32)
    tags = jnp.where(row == me, label, 0.0)
    for g in range(out_ref.shape[0]):
        out_ref[g, :groups, :] = acc
        out_ref[g, groups:, :] = tags


def margin_call(place, labels, columns, delta, delta_other, near, far):
    groups, seq_len, _ = columns.shape
    return pl.pallas_call(
        margin_kernel,
        in_specs=[SMEM, SMEM] + [VMEM] * 5,
        out_specs=VMEM,
        out_shape=jax.ShapeDtypeStruct((groups, 2 * groups, seq_len), f32),
        compiler_params=pltpu.CompilerParams(vmem_limit_bytes=VMEM_LIMIT),
    )(place, labels, columns, delta, delta_other, near, far)


def grad_kernel(place_ref, small_ref, columns_ref, near_ref, far_ref, grad_ref, margin_ref, slope_ref):
    groups, seq_len, depth = columns_ref.shape
    features = near_ref.shape[2]
    small = small_ref[0]
    for g in range(1, groups):
        small = small + small_ref[g]
    margin = small[:groups]
    margin_ref[...] = margin
    label = small[groups:, :1]
    total = jnp.sum(beta_scale * margin, axis=1, keepdims=True)
    weight = beta_scale * (1.0 / (1.0 + jnp.exp(-total)) - label)
    row = lax.broadcasted_iota(jnp.int32, weight.shape, 0)
    for swapped, read_ref in ((False, near_ref), (True, far_ref)):
        for j in range(4):
            seq = seq_of(place_ref, j, swapped)
            w = jnp.sum(jnp.where(row == seq, weight, 0.0), axis=0, keepdims=True)
            slope_ref[seq] = (w * read_ref[j].astype(f32)).astype(bf16)
    columns = columns_ref[...].reshape(groups * seq_len, depth)
    slope = slope_ref[...].reshape(groups * seq_len, features)
    grad = lax.dot_general(
        columns, slope, (((0,), (0,)), ((), ())), preferred_element_type=f32
    ).astype(bf16)
    y_hi, y_all = 2, 4
    part = depth // y_all
    for yh in range(y_hi):
        for yl in range(y_all // y_hi):
            at = (yl * y_hi + yh) * part
            grad_ref[yh * (y_all // y_hi) + yl] = grad[at : at + part]


def grad_call(place, small, columns, near, far):
    groups, seq_len, depth = columns.shape
    features = near.shape[2]
    return pl.pallas_call(
        grad_kernel,
        in_specs=[SMEM] + [VMEM] * 4,
        out_specs=[VMEM, VMEM],
        out_shape=[
            jax.ShapeDtypeStruct((4, depth // 4, features), bf16),
            jax.ShapeDtypeStruct((groups, seq_len), f32),
        ],
        scratch_shapes=[pltpu.VMEM((groups, seq_len, features), bf16)],
        compiler_params=pltpu.CompilerParams(vmem_limit_bytes=VMEM_LIMIT),
    )(place, small, columns, near, far)


def on_device(
    hidden, norm_gain, quant_ref, scale_ref, weight_prm, readout, lengths, bounds, labels
):
    seq_len, width = hidden.shape[1:]
    features = readout.shape[2]
    head_size = features // scale_ref.shape[0]
    steps_count = bounds.shape[1]
    group = lax.axis_size(GROUP)
    x, core, y_lo = lax.axis_index("x"), lax.axis_index("c"), lax.axis_index("yl")
    place = jnp.stack([x, core, y_lo]).astype(jnp.int32)
    pieces = norm_call(hidden[0], norm_gain[None], group)
    near = exchange(mask_call(lengths, readout[0], lax.axis_size("x")), ("x",))
    far = lax.ppermute(near, "c", [(0, 1), (1, 0)])
    columns = exchange(pieces, GROUP)
    expanded = jnp.repeat(scale_ref.T, head_size, axis=1)
    ref_local = (quant_ref.astype(f32) * expanded).astype(bf16)
    delta = (weight_prm.astype(f32) - ref_local.astype(f32)).astype(bf16)
    delta_other = lax.ppermute(delta, "yl", [(0, 1), (1, 0)])
    small = exchange(margin_call(place, labels, columns, delta, delta_other, near, far), GROUP)
    grad, margin = grad_call(place, small, columns, near, far)
    grad = wide_sum(exchange(grad, ("yh", "yl"))).astype(bf16)
    zl = lax.axis_size("zl")
    grad = grad.reshape(grad.shape[0], zl, features // zl).transpose(1, 0, 2)
    grad = wide_sum(exchange(grad, ("zl",))).astype(bf16)
    grad = wide_sum(spread(grad, ("zh",))).astype(bf16)
    grad = place_call(spread(grad, ("yh", "zl")), lax.axis_size("yh"))
    position = jnp.arange(seq_len, dtype=jnp.int32)
    reward = beta_scale * lax.dynamic_slice_in_dim(margin, 2 * x + core, 1, axis=0)
    step_index = jnp.sum((position[:, None] >= bounds[0][None, :]).astype(jnp.int32), axis=-1) - 1
    onehot = (step_index[:, None] == jnp.arange(steps_count)[None, :]).astype(f32)
    step_rewards = jnp.sum(reward[0][:, None] * onehot, axis=0)[None]
    return step_rewards, grad


def solution(mesh):
    fine = Mesh(mesh.devices.reshape(2, 4, 4, 2, 4, 2), AXES)
    every = REP + FSDP
    in_specs = (
        P(every, None, None),
        P(),
        P(FSDP, None),
        P(None, FSDP),
        P(FSDP, None),
        P(every, None, None),
        P(every),
        P(every, None),
        P(every),
    )
    out_specs = (P(every, None), P(FSDP, None))
    return jax.shard_map(
        on_device, mesh=fine, in_specs=in_specs, out_specs=out_specs, check_vma=False
    )
```

```python
import jax
import jax.numpy as jnp
from jax import lax
from jax.experimental import pallas as pl
from jax.experimental.pallas import tpu as pltpu
from jax.sharding import Mesh, PartitionSpec as P

epsilon = 1e-06
beta_scale = 0.05

AXES = ("yh", "zh", "zl", "yl", "x", "c")
REP = ("yh", "zh", "zl")
FSDP = ("yl", "x", "c")
GROUP = ("x", "c")
OFFSETS = (0, -1, 1, 2)
VMEM_LIMIT = 24 * 1024 * 1024
VMEM = pl.BlockSpec(memory_space=pltpu.VMEM)
SMEM = pl.BlockSpec(memory_space=pltpu.SMEM)
f32, bf16 = jnp.float32, jnp.bfloat16


def exchange(pieces, axes):
    return lax.all_to_all(pieces, axes, 0, 0, tiled=False)


def spread(block, axes):
    count = lax.axis_size(axes)
    return exchange(jnp.broadcast_to(block[None], (count,) + block.shape), axes)


def wide_sum(parts):
    total = parts[0].astype(f32)
    for k in range(1, parts.shape[0]):
        total = total + parts[k].astype(f32)
    return total


def norm_kernel(lengths_ref, hidden_ref, gain_ref, readout_ref, pieces_ref, masked_ref):
    block, width = hidden_ref.shape
    groups, _, share = pieces_ref.shape
    part = share // 2
    wide = hidden_ref[...].astype(f32)
    mean_square = jnp.sum(wide * wide, axis=-1, keepdims=True) * (1.0 / width)
    scale = lax.rsqrt(mean_square + epsilon)
    normed = (wide * scale * gain_ref[...]).astype(bf16)
    for g in range(groups):
        starts = [(yl * groups + g) * part for yl in range(2)]
        pieces_ref[g] = jnp.concatenate([normed[:, at : at + part] for at in starts], axis=1)
    position = lax.broadcasted_iota(jnp.int32, readout_ref.shape, 0) + pl.program_id(0) * block
    read = readout_ref[...].astype(f32)
    masked_ref[...] = jnp.where(position < lengths_ref[0], read, 0.0).astype(bf16)


def norm_call(lengths, hidden, gain, readout, groups):
    seq_len, width = hidden.shape
    features = readout.shape[1]
    share = width // groups
    block = 64
    return pl.pallas_call(
        norm_kernel,
        grid=(seq_len // block,),
        in_specs=[
            SMEM,
            pl.BlockSpec((block, width), lambda i: (i, 0)),
            pl.BlockSpec((1, width), lambda i: (0, 0)),
            pl.BlockSpec((block, features), lambda i: (i, 0)),
        ],
        out_specs=[
            pl.BlockSpec((groups, block, share), lambda i: (0, i, 0)),
            pl.BlockSpec((block, features), lambda i: (i, 0)),
        ],
        out_shape=[
            jax.ShapeDtypeStruct((groups, seq_len, share), bf16),
            jax.ShapeDtypeStruct((seq_len, features), bf16),
        ],
        compiler_params=pltpu.CompilerParams(vmem_limit_bytes=60 * 1024 * 1024),
    )(lengths, hidden, gain, readout)


def place_kernel(pieces_ref, out_ref):
    for k in range(pieces_ref.shape[0]):
        out_ref[:, 128 * k : 128 * (k + 1)] = pieces_ref[k].astype(f32)


def place_call(pieces, halves):
    count, part, lanes = pieces.shape
    across = count // halves
    return pl.pallas_call(
        place_kernel,
        grid=(halves,),
        in_specs=[pl.BlockSpec((across, part, lanes), lambda i: (i, 0, 0))],
        out_specs=pl.BlockSpec((part, across * lanes), lambda i: (i, 0)),
        out_shape=jax.ShapeDtypeStruct((halves * part, across * lanes), f32),
        compiler_params=pltpu.CompilerParams(vmem_limit_bytes=VMEM_LIMIT),
    )(pieces)


def seq_of(place_ref, j, swapped):
    x_from = lax.rem(place_ref[0] + (OFFSETS[j] + 4), 4)
    core = place_ref[2]
    return 2 * x_from + (1 - core if swapped else core)


def add_margins(acc, place_ref, columns_ref, delta, reads, swapped):
    row = lax.broadcasted_iota(jnp.int32, acc.shape, 0)
    for j in range(4):
        seq = seq_of(place_ref, j, swapped)
        value = jnp.dot(columns_ref[seq], delta, preferred_element_type=f32)
        prod = value * reads[j].astype(f32)
        part = prod[:, :128]
        for k in range(1, prod.shape[1] // 128):
            part = part + prod[:, 128 * k : 128 * (k + 1)]
        line = jnp.sum(part.T, axis=0, keepdims=True)
        acc = jnp.where(row == seq, line, acc)
    return acc


def margin_kernel(
    place_ref, tags_ref, own, other, columns_ref, n0, n1, n2, n3, f0, f3, out_ref, delta_ref
):
    groups, seq_len, share = columns_ref.shape
    delta_ref[place_ref[1]] = own[...]
    delta_ref[1 - place_ref[1]] = other[...]
    delta = delta_ref[...].reshape(share, delta_ref.shape[2])
    row = lax.broadcasted_iota(jnp.int32, (2 * groups, seq_len), 0)
    me = seq_of(place_ref, 0, False)
    acc = jnp.where(row == me + groups, tags_ref[0].astype(f32), 0.0)
    near = [ref[...] for ref in (n0, n1, n2, n3)]
    far = [f0[...]] + [f3[j] for j in range(3)]
    acc = add_margins(acc, place_ref, columns_ref, delta, near, False)
    acc = add_margins(acc, place_ref, columns_ref, delta, far, True)
    for g in range(out_ref.shape[0]):
        out_ref[g] = acc


def margin_call(place, labels, deltas, columns, near, far):
    groups, seq_len, _ = columns.shape
    return pl.pallas_call(
        margin_kernel,
        in_specs=[SMEM, SMEM] + [VMEM] * 9,
        out_specs=VMEM,
        out_shape=jax.ShapeDtypeStruct((groups, 2 * groups, seq_len), f32),
        scratch_shapes=[pltpu.VMEM((2,) + deltas[0].shape, bf16)],
        compiler_params=pltpu.CompilerParams(vmem_limit_bytes=VMEM_LIMIT),
    )(place, labels, *deltas, columns, *near, *far)


def grad_kernel(
    place_ref, small_ref, columns_ref, n0, n1, n2, n3, f0, f3, grad_ref, margin_ref, slope_ref
):
    groups, seq_len, share = columns_ref.shape
    small = small_ref[0]
    for g in range(1, groups):
        small = small + small_ref[g]
    margin = small[:groups]
    margin_ref[...] = margin
    label = small[groups:, :1]
    total = jnp.sum(beta_scale * margin, axis=1, keepdims=True)
    weight = beta_scale * (1.0 / (1.0 + jnp.exp(-total)) - label)
    row = lax.broadcasted_iota(jnp.int32, weight.shape, 0)
    near = [ref[...] for ref in (n0, n1, n2, n3)]
    far = [f0[...]] + [f3[j] for j in range(3)]
    for swapped, reads in ((False, near), (True, far)):
        for j in range(4):
            seq = seq_of(place_ref, j, swapped)
            w = jnp.sum(jnp.where(row == seq, weight, 0.0), axis=0, keepdims=True)
            slope_ref[seq] = (w * reads[j].astype(f32)).astype(bf16)
    columns = columns_ref[...].reshape(groups * seq_len, share)
    slope = slope_ref[...].reshape(groups * seq_len, slope_ref.shape[2])
    grad = lax.dot_general(
        columns, slope, (((0,), (0,)), ((), ())), preferred_element_type=f32
    ).astype(bf16)
    part = grad_ref.shape[1]
    for yh in range(2):
        for yl in range(2):
            at = (2 * yl + yh) * part
            grad_ref[2 * yh + yl] = grad[at : at + part]


def grad_call(place, small, columns, near, far):
    groups, seq_len, share = columns.shape
    features = near[0].shape[1]
    return pl.pallas_call(
        grad_kernel,
        in_specs=[SMEM] + [VMEM] * 8,
        out_specs=[VMEM, VMEM],
        out_shape=[
            jax.ShapeDtypeStruct((4, share // 4, features), bf16),
            jax.ShapeDtypeStruct((groups, seq_len), f32),
        ],
        scratch_shapes=[pltpu.VMEM((groups, seq_len, features), bf16)],
        compiler_params=pltpu.CompilerParams(vmem_limit_bytes=VMEM_LIMIT),
    )(place, small, columns, *near, *far)


def shifted(block, axes):
    pairs = [[(i, (i - shift) % 4) for i in range(4)] for shift in OFFSETS[1:]]
    return [block] + [lax.ppermute(block, axes, pair) for pair in pairs]


def on_device(
    hidden, norm_gain, quant_ref, scale_ref, weight_prm, readout, lengths, bounds, labels
):
    seq_len, width = hidden.shape[1:]
    features = readout.shape[2]
    head_size = features // scale_ref.shape[0]
    steps_count = bounds.shape[1]
    group = lax.axis_size(GROUP)
    x, y_lo, core = lax.axis_index("x"), lax.axis_index("yl"), lax.axis_index("c")
    me = 2 * x + core
    place = jnp.stack([x, y_lo, core]).astype(jnp.int32)
    swap = [(0, 1), (1, 0)]
    pieces, masked = norm_call(lengths, hidden[0], norm_gain[None], readout[0], group)
    columns = exchange(pieces, GROUP)
    expanded = jnp.repeat(scale_ref.T, head_size, axis=1)
    ref_local = (quant_ref.astype(f32) * expanded).astype(bf16)
    delta = (weight_prm.astype(f32) - ref_local.astype(f32)).astype(bf16)
    delta_other = lax.ppermute(delta, "yl", swap)
    near = shifted(masked, ("x",))
    far_own = lax.ppermute(masked, "c", swap)
    moved = jnp.stack(near[1:])
    moved, delta_other, far_own = lax.optimization_barrier((moved, delta_other, far_own))
    far = [far_own, lax.ppermute(moved, "c", swap)]
    deltas = [delta, delta_other]
    small = exchange(margin_call(place, labels, deltas, columns, near, far), GROUP)
    grad, margin = grad_call(place, small, columns, near, far)
    grad = wide_sum(exchange(grad, ("yh", "yl"))).astype(bf16)
    zl = lax.axis_size("zl")
    grad = grad.reshape(grad.shape[0], zl, features // zl).transpose(1, 0, 2)
    grad = wide_sum(exchange(grad, ("zl",))).astype(bf16)
    grad = wide_sum(spread(grad, ("zh",))).astype(bf16)
    grad = place_call(spread(grad, ("yh", "zl")), lax.axis_size("yh"))
    position = jnp.arange(seq_len, dtype=jnp.int32)
    reward = beta_scale * lax.dynamic_slice_in_dim(margin, me, 1, axis=0)
    step_index = jnp.sum((position[:, None] >= bounds[0][None, :]).astype(jnp.int32), axis=-1) - 1
    onehot = (step_index[:, None] == jnp.arange(steps_count)[None, :]).astype(f32)
    step_rewards = jnp.sum(reward[0][:, None] * onehot, axis=0)[None]
    return step_rewards, grad


def solution(mesh):
    fine = Mesh(mesh.devices.reshape(2, 4, 4, 2, 4, 2), AXES)
    every = REP + FSDP
    in_specs = (
        P(every, None, None),
        P(),
        P(FSDP, None),
        P(None, FSDP),
        P(FSDP, None),
        P(every, None, None),
        P(every),
        P(every, None),
        P(every),
    )
    out_specs = (P(every, None), P(FSDP, None))
    return jax.shard_map(
        on_device, mesh=fine, in_specs=in_specs, out_specs=out_specs, check_vma=False
    )
```

```python
import jax
import jax.numpy as jnp
from jax import lax
from jax.experimental import pallas as pl
from jax.experimental.pallas import tpu as pltpu
from jax.sharding import Mesh, PartitionSpec as P

epsilon = 1e-06
beta_scale = 0.05

AXES = ("yh", "zh", "zl", "yl", "x", "c")
REP = ("yh", "zh", "zl")
FSDP = ("yl", "x", "c")
GROUP = ("x", "c")
OFFSETS = (0, -1, 1, 2)
VMEM_LIMIT = 24 * 1024 * 1024
VMEM = pl.BlockSpec(memory_space=pltpu.VMEM)
SMEM = pl.BlockSpec(memory_space=pltpu.SMEM)
f32, bf16 = jnp.float32, jnp.bfloat16


def exchange(pieces, axes):
    return lax.all_to_all(pieces, axes, 0, 0, tiled=False)


def spread(block, axes):
    count = lax.axis_size(axes)
    return exchange(jnp.broadcast_to(block[None], (count,) + block.shape), axes)


def wide_sum(parts):
    total = parts[0].astype(f32)
    for k in range(1, parts.shape[0]):
        total = total + parts[k].astype(f32)
    return total


def norm_kernel(hidden_ref, gain_ref, pieces_ref):
    width = hidden_ref.shape[1]
    groups, _, share = pieces_ref.shape
    part = share // 2
    wide = hidden_ref[...].astype(f32)
    mean_square = jnp.sum(wide * wide, axis=-1, keepdims=True) * (1.0 / width)
    scale = lax.rsqrt(mean_square + epsilon)
    normed = (wide * scale * gain_ref[...]).astype(bf16)
    for g in range(groups):
        starts = [(yl * groups + g) * part for yl in range(2)]
        pieces_ref[g] = jnp.concatenate([normed[:, at : at + part] for at in starts], axis=1)


def norm_call(hidden, gain, groups):
    seq_len, width = hidden.shape
    share = width // groups
    block = 64
    return pl.pallas_call(
        norm_kernel,
        grid=(seq_len // block,),
        in_specs=[
            pl.BlockSpec((block, width), lambda i: (i, 0)),
            pl.BlockSpec((1, width), lambda i: (0, 0)),
        ],
        out_specs=pl.BlockSpec((groups, block, share), lambda i: (0, i, 0)),
        out_shape=jax.ShapeDtypeStruct((groups, seq_len, share), bf16),
        compiler_params=pltpu.CompilerParams(vmem_limit_bytes=60 * 1024 * 1024),
    )(hidden, gain)


def place_kernel(pieces_ref, out_ref):
    for k in range(pieces_ref.shape[0]):
        out_ref[:, 128 * k : 128 * (k + 1)] = pieces_ref[k].astype(f32)


def place_call(pieces, halves):
    count, part, lanes = pieces.shape
    across = count // halves
    return pl.pallas_call(
        place_kernel,
        grid=(halves,),
        in_specs=[pl.BlockSpec((across, part, lanes), lambda i: (i, 0, 0))],
        out_specs=pl.BlockSpec((part, across * lanes), lambda i: (i, 0)),
        out_shape=jax.ShapeDtypeStruct((halves * part, across * lanes), f32),
        compiler_params=pltpu.CompilerParams(vmem_limit_bytes=VMEM_LIMIT),
    )(pieces)


def seq_of(place_ref, j, swapped):
    x_from = lax.rem(place_ref[0] + (OFFSETS[j] + 4), 4)
    core = place_ref[2]
    return 2 * x_from + (1 - core if swapped else core)


def add_margins(acc, place_ref, columns_ref, delta, reads, swapped):
    row = lax.broadcasted_iota(jnp.int32, acc.shape, 0)
    for j in range(4):
        seq = seq_of(place_ref, j, swapped)
        value = jnp.dot(columns_ref[seq], delta, preferred_element_type=f32)
        prod = value * reads[j].astype(f32)
        part = prod[:, :128]
        for k in range(1, prod.shape[1] // 128):
            part = part + prod[:, 128 * k : 128 * (k + 1)]
        line = jnp.sum(part.T, axis=0, keepdims=True)
        acc = jnp.where(row == seq, line, acc)
    return acc


def near_kernel(place_ref, tags_ref, delta_ref, columns_ref, n0, n1, n2, n3, acc_ref):
    groups, seq_len, _ = columns_ref.shape
    row = lax.broadcasted_iota(jnp.int32, acc_ref.shape, 0)
    lane = lax.broadcasted_iota(jnp.int32, acc_ref.shape, 1)
    me = seq_of(place_ref, 0, False)
    tags = jnp.where(lane < seq_len // 2, tags_ref[0], tags_ref[1]).astype(f32)
    acc = jnp.where(row == me + groups, tags, 0.0)
    reads = [ref[...] for ref in (n0, n1, n2, n3)]
    acc_ref[...] = add_margins(acc, place_ref, columns_ref, delta_ref[...], reads, False)


def far_kernel(place_ref, acc_ref, delta_ref, columns_ref, f0, f3, out_ref):
    reads = [f0[...]] + [f3[j] for j in range(3)]
    acc = add_margins(acc_ref[...], place_ref, columns_ref, delta_ref[...], reads, True)
    for g in range(out_ref.shape[0]):
        out_ref[g] = acc


def margin_call(place, tags, delta, columns, near, far):
    groups, seq_len, _ = columns.shape
    params = pltpu.CompilerParams(vmem_limit_bytes=VMEM_LIMIT)
    acc = pl.pallas_call(
        near_kernel,
        in_specs=[SMEM, SMEM] + [VMEM] * 6,
        out_specs=VMEM,
        out_shape=jax.ShapeDtypeStruct((2 * groups, seq_len), f32),
        compiler_params=params,
    )(place, tags, delta, columns, *near)
    return pl.pallas_call(
        far_kernel,
        in_specs=[SMEM] + [VMEM] * 5,
        out_specs=VMEM,
        out_shape=jax.ShapeDtypeStruct((groups, 2 * groups, seq_len), f32),
        compiler_params=params,
    )(place, acc, delta, columns, *far)


def grad_kernel(
    place_ref, small_ref, columns_ref, n0, n1, n2, n3, f0, f3, grad_ref, margin_ref, slope_ref
):
    groups, seq_len, share = columns_ref.shape
    small = small_ref[0]
    for g in range(1, groups):
        small = small + small_ref[g]
    label, length = small[groups:, :1], small[groups:, seq_len - 1 :]
    lane = lax.broadcasted_iota(jnp.int32, (groups, seq_len), 1).astype(f32)
    margin = jnp.where(lane < length, small[:groups], 0.0)
    margin_ref[...] = margin
    total = jnp.sum(beta_scale * margin, axis=1, keepdims=True)
    weight = beta_scale * (1.0 / (1.0 + jnp.exp(-total)) - label)
    row = lax.broadcasted_iota(jnp.int32, weight.shape, 0)
    position = lax.broadcasted_iota(jnp.int32, (seq_len, 1), 0).astype(f32)
    near = [ref[...] for ref in (n0, n1, n2, n3)]
    far = [f0[...]] + [f3[j] for j in range(3)]
    for swapped, reads in ((False, near), (True, far)):
        for j in range(4):
            seq = seq_of(place_ref, j, swapped)
            w = jnp.sum(jnp.where(row == seq, weight, 0.0), axis=0, keepdims=True)
            live = position < jnp.sum(jnp.where(row == seq, length, 0.0), axis=0, keepdims=True)
            slope_ref[seq] = (jnp.where(live, w, 0.0) * reads[j].astype(f32)).astype(bf16)
    columns = columns_ref[...].reshape(groups * seq_len, share)
    slope = slope_ref[...].reshape(groups * seq_len, slope_ref.shape[2])
    grad = lax.dot_general(
        columns, slope, (((0,), (0,)), ((), ())), preferred_element_type=f32
    ).astype(bf16)
    part = grad_ref.shape[1]
    for yh in range(2):
        for yl in range(2):
            at = (2 * yl + yh) * part
            grad_ref[2 * yh + yl] = grad[at : at + part]


def grad_call(place, small, columns, near, far):
    groups, seq_len, share = columns.shape
    features = near[0].shape[1]
    return pl.pallas_call(
        grad_kernel,
        in_specs=[SMEM] + [VMEM] * 8,
        out_specs=[VMEM, VMEM],
        out_shape=[
            jax.ShapeDtypeStruct((4, share // 4, features), bf16),
            jax.ShapeDtypeStruct((groups, seq_len), f32),
        ],
        scratch_shapes=[pltpu.VMEM((groups, seq_len, features), bf16)],
        compiler_params=pltpu.CompilerParams(vmem_limit_bytes=VMEM_LIMIT),
    )(place, small, columns, *near, *far)


def shifted(block, axes):
    pairs = [[(i, (i - shift) % 4) for i in range(4)] for shift in OFFSETS[1:]]
    return [block] + [lax.ppermute(block, axes, pair) for pair in pairs]


def on_device(
    hidden, norm_gain, quant_ref, scale_ref, weight_prm, readout, lengths, bounds, labels
):
    seq_len, width = hidden.shape[1:]
    features = readout.shape[2]
    head_size = features // scale_ref.shape[0]
    steps_count = bounds.shape[1]
    group = lax.axis_size(GROUP)
    x, y_lo, core = lax.axis_index("x"), lax.axis_index("yl"), lax.axis_index("c")
    me = 2 * x + core
    place = jnp.stack([x, y_lo, core]).astype(jnp.int32)
    swap = [(0, 1), (1, 0)]
    pieces = norm_call(hidden[0], norm_gain[None], group)
    columns = exchange(pieces, GROUP)
    expanded = jnp.repeat(scale_ref.T, head_size, axis=1)
    ref_local = (quant_ref.astype(f32) * expanded).astype(bf16)
    delta = (weight_prm.astype(f32) - ref_local.astype(f32)).astype(bf16)
    delta_other = lax.ppermute(delta, "yl", swap)
    own, _, _ = lax.optimization_barrier((readout[0], pieces, delta))
    pair = [jnp.where(y_lo == k, delta, delta_other) for k in range(2)]
    delta = jnp.concatenate(pair, axis=0)
    near = shifted(own, ("x",))
    far_own = lax.ppermute(own, "c", swap)
    tags = jnp.concatenate([labels, lengths])
    moved = jnp.stack(near[1:])
    moved, delta, far_own, place, tags = lax.optimization_barrier(
        (moved, delta, far_own, place, tags)
    )
    far = [far_own, lax.ppermute(moved, "c", swap)]
    small = exchange(margin_call(place, tags, delta, columns, near, far), GROUP)
    grad, margin = grad_call(place, small, columns, near, far)
    grad = wide_sum(exchange(grad, ("yh", "yl"))).astype(bf16)
    zl = lax.axis_size("zl")
    grad = grad.reshape(grad.shape[0], zl, features // zl).transpose(1, 0, 2)
    grad = wide_sum(exchange(grad, ("zl",))).astype(bf16)
    grad = wide_sum(spread(grad, ("zh",))).astype(bf16)
    grad = place_call(spread(grad, ("yh", "zl")), lax.axis_size("yh"))
    position = jnp.arange(seq_len, dtype=jnp.int32)
    reward = beta_scale * lax.dynamic_slice_in_dim(margin, me, 1, axis=0)
    step_index = jnp.sum((position[:, None] >= bounds[0][None, :]).astype(jnp.int32), axis=-1) - 1
    onehot = (step_index[:, None] == jnp.arange(steps_count)[None, :]).astype(f32)
    step_rewards = jnp.sum(reward[0][:, None] * onehot, axis=0)[None]
    return step_rewards, grad


def solution(mesh):
    fine = Mesh(mesh.devices.reshape(2, 4, 4, 2, 4, 2), AXES)
    every = REP + FSDP
    in_specs = (
        P(every, None, None),
        P(),
        P(FSDP, None),
        P(None, FSDP),
        P(FSDP, None),
        P(every, None, None),
        P(every),
        P(every, None),
        P(every),
    )
    out_specs = (P(every, None), P(FSDP, None))
    return jax.shard_map(
        on_device, mesh=fine, in_specs=in_specs, out_specs=out_specs, check_vma=False
    )
```

```python
import jax
import jax.numpy as jnp
from jax import lax
from jax.experimental import pallas as pl
from jax.experimental.pallas import tpu as pltpu
from jax.sharding import Mesh, PartitionSpec as P

epsilon = 1e-06
beta_scale = 0.05

AXES = ("yh", "zh", "zl", "yl", "x", "c")
REP = ("yh", "zh", "zl")
FSDP = ("yl", "x", "c")
GROUP = ("x", "c")
OFFSETS = (0, -1, 1, 2)
VMEM_LIMIT = 24 * 1024 * 1024
VMEM = pl.BlockSpec(memory_space=pltpu.VMEM)
SMEM = pl.BlockSpec(memory_space=pltpu.SMEM)
f32, bf16 = jnp.float32, jnp.bfloat16


def exchange(pieces, axes):
    return lax.all_to_all(pieces, axes, 0, 0, tiled=False)


def spread(block, axes):
    count = lax.axis_size(axes)
    return exchange(jnp.broadcast_to(block[None], (count,) + block.shape), axes)


def wide_sum(parts):
    total = parts[0].astype(f32)
    for k in range(1, parts.shape[0]):
        total = total + parts[k].astype(f32)
    return total


def norm_kernel(hidden_ref, gain_ref, pieces_ref):
    width = hidden_ref.shape[1]
    groups, _, share = pieces_ref.shape
    part = share // 2
    wide = hidden_ref[...].astype(f32)
    mean_square = jnp.sum(wide * wide, axis=-1, keepdims=True) * (1.0 / width)
    scale = lax.rsqrt(mean_square + epsilon)
    normed = (wide * scale * gain_ref[...]).astype(bf16)
    for g in range(groups):
        starts = [(yl * groups + g) * part for yl in range(2)]
        pieces_ref[g] = jnp.concatenate([normed[:, at : at + part] for at in starts], axis=1)


def norm_call(hidden, gain, groups):
    seq_len, width = hidden.shape
    share = width // groups
    block = 64
    return pl.pallas_call(
        norm_kernel,
        grid=(seq_len // block,),
        in_specs=[
            pl.BlockSpec((block, width), lambda i: (i, 0)),
            pl.BlockSpec((1, width), lambda i: (0, 0)),
        ],
        out_specs=pl.BlockSpec((groups, block, share), lambda i: (0, i, 0)),
        out_shape=jax.ShapeDtypeStruct((groups, seq_len, share), bf16),
        compiler_params=pltpu.CompilerParams(vmem_limit_bytes=60 * 1024 * 1024),
    )(hidden, gain)


def place_kernel(pieces_ref, out_ref):
    for k in range(pieces_ref.shape[0]):
        out_ref[:, 128 * k : 128 * (k + 1)] = pieces_ref[k].astype(f32)


def place_call(pieces, halves):
    count, part, lanes = pieces.shape
    across = count // halves
    return pl.pallas_call(
        place_kernel,
        grid=(halves,),
        in_specs=[pl.BlockSpec((across, part, lanes), lambda i: (i, 0, 0))],
        out_specs=pl.BlockSpec((part, across * lanes), lambda i: (i, 0)),
        out_shape=jax.ShapeDtypeStruct((halves * part, across * lanes), f32),
        compiler_params=pltpu.CompilerParams(vmem_limit_bytes=VMEM_LIMIT),
    )(pieces)


def seq_of(place_ref, j, swapped):
    x_from = lax.rem(place_ref[0] + (OFFSETS[j] + 4), 4)
    core = place_ref[2]
    return 2 * x_from + (1 - core if swapped else core)


def add_margins(acc, place_ref, columns_ref, delta, reads, swapped):
    row = lax.broadcasted_iota(jnp.int32, acc.shape, 0)
    for j in range(4):
        seq = seq_of(place_ref, j, swapped)
        value = jnp.dot(columns_ref[seq], delta, preferred_element_type=f32)
        prod = value * reads[j].astype(f32)
        part = prod[:, :128]
        for k in range(1, prod.shape[1] // 128):
            part = part + prod[:, 128 * k : 128 * (k + 1)]
        line = jnp.sum(part.T, axis=0, keepdims=True)
        acc = jnp.where(row == seq, line, acc)
    return acc


def near_kernel(place_ref, tags_ref, delta_ref, columns_ref, n0, n1, n2, n3, acc_ref):
    groups, seq_len, _ = columns_ref.shape
    row = lax.broadcasted_iota(jnp.int32, acc_ref.shape, 0)
    lane = lax.broadcasted_iota(jnp.int32, acc_ref.shape, 1)
    me = seq_of(place_ref, 0, False)
    tags = jnp.where(lane < seq_len // 2, tags_ref[0], tags_ref[1]).astype(f32)
    acc = jnp.where(row == me + groups, tags, 0.0)
    reads = [ref[...] for ref in (n0, n1, n2, n3)]
    acc_ref[...] = add_margins(acc, place_ref, columns_ref, delta_ref[...], reads, False)


def far_kernel(place_ref, acc_ref, delta_ref, columns_ref, f0, f3, out_ref):
    reads = [f0[...]] + [f3[j] for j in range(3)]
    acc = add_margins(acc_ref[...], place_ref, columns_ref, delta_ref[...], reads, True)
    for g in range(out_ref.shape[0]):
        out_ref[g] = acc


def margin_call(place, tags, delta, columns, near, far):
    groups, seq_len, _ = columns.shape
    params = pltpu.CompilerParams(vmem_limit_bytes=VMEM_LIMIT)
    acc = pl.pallas_call(
        near_kernel,
        in_specs=[SMEM, SMEM] + [VMEM] * 6,
        out_specs=VMEM,
        out_shape=jax.ShapeDtypeStruct((2 * groups, seq_len), f32),
        compiler_params=params,
    )(place, tags, delta, columns, *near)
    return pl.pallas_call(
        far_kernel,
        in_specs=[SMEM] + [VMEM] * 5,
        out_specs=VMEM,
        out_shape=jax.ShapeDtypeStruct((groups, 2 * groups, seq_len), f32),
        compiler_params=params,
    )(place, acc, delta, columns, *far)


def grad_kernel(
    place_ref, small_ref, columns_ref, n0, n1, n2, n3, f0, f3, grad_ref, margin_ref, slope_ref
):
    groups, seq_len, share = columns_ref.shape
    small = small_ref[0]
    for g in range(1, groups):
        small = small + small_ref[g]
    label, length = small[groups:, :1], small[groups:, seq_len - 1 :]
    lane = lax.broadcasted_iota(jnp.int32, (groups, seq_len), 1).astype(f32)
    margin = jnp.where(lane < length, small[:groups], 0.0)
    margin_ref[...] = margin
    total = jnp.sum(beta_scale * margin, axis=1, keepdims=True)
    weight = beta_scale * (1.0 / (1.0 + jnp.exp(-total)) - label)
    row = lax.broadcasted_iota(jnp.int32, weight.shape, 0)
    position = lax.broadcasted_iota(jnp.int32, (seq_len, 1), 0).astype(f32)
    near = [ref[...] for ref in (n0, n1, n2, n3)]
    far = [f0[...]] + [f3[j] for j in range(3)]
    for swapped, reads in ((False, near), (True, far)):
        for j in range(4):
            seq = seq_of(place_ref, j, swapped)
            w = jnp.sum(jnp.where(row == seq, weight, 0.0), axis=0, keepdims=True)
            live = position < jnp.sum(jnp.where(row == seq, length, 0.0), axis=0, keepdims=True)
            slope_ref[seq] = (jnp.where(live, w, 0.0) * reads[j].astype(f32)).astype(bf16)
    columns = columns_ref[...].reshape(groups * seq_len, share)
    slope = slope_ref[...].reshape(groups * seq_len, slope_ref.shape[2])
    grad = lax.dot_general(
        columns, slope, (((0,), (0,)), ((), ())), preferred_element_type=f32
    ).astype(bf16)
    part = grad_ref.shape[1]
    for yh in range(2):
        for yl in range(2):
            at = (2 * yl + yh) * part
            grad_ref[2 * yh + yl] = grad[at : at + part]


def grad_call(place, small, columns, near, far):
    groups, seq_len, share = columns.shape
    features = near[0].shape[1]
    return pl.pallas_call(
        grad_kernel,
        in_specs=[SMEM] + [VMEM] * 8,
        out_specs=[VMEM, VMEM],
        out_shape=[
            jax.ShapeDtypeStruct((4, share // 4, features), bf16),
            jax.ShapeDtypeStruct((groups, seq_len), f32),
        ],
        scratch_shapes=[pltpu.VMEM((groups, seq_len, features), bf16)],
        compiler_params=pltpu.CompilerParams(vmem_limit_bytes=VMEM_LIMIT),
    )(place, small, columns, *near, *far)


def shifted(block, axes):
    pairs = [[(i, (i - shift) % 4) for i in range(4)] for shift in OFFSETS[1:]]
    return [block] + [lax.ppermute(block, axes, pair) for pair in pairs]


def on_device(
    hidden, norm_gain, quant_ref, scale_ref, weight_prm, readout, lengths, bounds, labels
):
    seq_len, width = hidden.shape[1:]
    features = readout.shape[2]
    head_size = features // scale_ref.shape[0]
    steps_count = bounds.shape[1]
    group = lax.axis_size(GROUP)
    x, y_lo, core = lax.axis_index("x"), lax.axis_index("yl"), lax.axis_index("c")
    me = 2 * x + core
    place = jnp.stack([x, y_lo, core]).astype(jnp.int32)
    swap = [(0, 1), (1, 0)]
    pieces = norm_call(hidden[0], norm_gain[None], group)
    columns = exchange(pieces, GROUP)
    expanded = jnp.repeat(scale_ref.T, head_size, axis=1)
    ref_local = (quant_ref.astype(f32) * expanded).astype(bf16)
    delta = (weight_prm.astype(f32) - ref_local.astype(f32)).astype(bf16)
    delta_other = lax.ppermute(delta, "yl", swap)
    own, _, _ = lax.optimization_barrier((readout[0], pieces, delta))
    pair = [jnp.where(y_lo == k, delta, delta_other) for k in range(2)]
    delta = jnp.concatenate(pair, axis=0)
    near = shifted(own, ("x",))
    far_own = lax.ppermute(own, "c", swap)
    tags = jnp.concatenate([labels, lengths])
    moved = jnp.stack(near[1:])
    moved, delta, far_own, place, tags = lax.optimization_barrier(
        (moved, delta, far_own, place, tags)
    )
    far = [far_own, lax.ppermute(moved, "c", swap)]
    small = exchange(margin_call(place, tags, delta, columns, near, far), GROUP)
    grad, margin = grad_call(place, small, columns, near, far)
    grad = wide_sum(exchange(grad, ("yh", "yl"))).astype(bf16)
    zl = lax.axis_size("zl")
    grad = grad.reshape(grad.shape[0], zl, features // zl).transpose(1, 0, 2)
    grad = wide_sum(exchange(grad, ("zl",))).astype(bf16)
    grad = wide_sum(lax.all_gather(grad, "zh")).astype(bf16)
    grad = place_call(spread(grad, ("yh", "zl")), lax.axis_size("yh"))
    position = jnp.arange(seq_len, dtype=jnp.int32)
    reward = beta_scale * lax.dynamic_slice_in_dim(margin, me, 1, axis=0)
    step_index = jnp.sum((position[:, None] >= bounds[0][None, :]).astype(jnp.int32), axis=-1) - 1
    onehot = (step_index[:, None] == jnp.arange(steps_count)[None, :]).astype(f32)
    step_rewards = jnp.sum(reward[0][:, None] * onehot, axis=0)[None]
    return step_rewards, grad


def solution(mesh):
    fine = Mesh(mesh.devices.reshape(2, 4, 4, 2, 4, 2), AXES)
    every = REP + FSDP
    in_specs = (
        P(every, None, None),
        P(),
        P(FSDP, None),
        P(None, FSDP),
        P(FSDP, None),
        P(every, None, None),
        P(every),
        P(every, None),
        P(every),
    )
    out_specs = (P(every, None), P(FSDP, None))
    return jax.shard_map(
        on_device, mesh=fine, in_specs=in_specs, out_specs=out_specs, check_vma=False
    )
```

```python
import jax
import jax.numpy as jnp
from jax import lax
from jax.experimental import pallas as pl
from jax.experimental.pallas import tpu as pltpu
from jax.sharding import Mesh, PartitionSpec as P

epsilon = 1e-06
beta_scale = 0.05

AXES = ("yh", "zh", "zl", "yl", "x", "c")
REP = ("yh", "zh", "zl")
FSDP = ("yl", "x", "c")
GROUP = ("x", "c")
OFFSETS = (0, -1, 1, 2)
VMEM_LIMIT = 24 * 1024 * 1024
VMEM = pl.BlockSpec(memory_space=pltpu.VMEM)
SMEM = pl.BlockSpec(memory_space=pltpu.SMEM)
f32, bf16 = jnp.float32, jnp.bfloat16


def exchange(pieces, axes):
    return lax.all_to_all(pieces, axes, 0, 0, tiled=False)


def spread(block, axes):
    count = lax.axis_size(axes)
    return exchange(jnp.broadcast_to(block[None], (count,) + block.shape), axes)


def wide_sum(parts):
    total = parts[0].astype(f32)
    for k in range(1, parts.shape[0]):
        total = total + parts[k].astype(f32)
    return total


def norm_kernel(hidden_ref, gain_ref, pieces_ref):
    width = hidden_ref.shape[1]
    groups, _, share = pieces_ref.shape
    part = share // 2
    wide = hidden_ref[...].astype(f32)
    mean_square = jnp.sum(wide * wide, axis=-1, keepdims=True) * (1.0 / width)
    scale = lax.rsqrt(mean_square + epsilon)
    normed = (wide * scale * gain_ref[...]).astype(bf16)
    for g in range(groups):
        starts = [(yl * groups + g) * part for yl in range(2)]
        pieces_ref[g] = jnp.concatenate([normed[:, at : at + part] for at in starts], axis=1)


def norm_call(hidden, gain, groups):
    seq_len, width = hidden.shape
    share = width // groups
    block = 64
    return pl.pallas_call(
        norm_kernel,
        grid=(seq_len // block,),
        in_specs=[
            pl.BlockSpec((block, width), lambda i: (i, 0)),
            pl.BlockSpec((1, width), lambda i: (0, 0)),
        ],
        out_specs=pl.BlockSpec((groups, block, share), lambda i: (0, i, 0)),
        out_shape=jax.ShapeDtypeStruct((groups, seq_len, share), bf16),
        compiler_params=pltpu.CompilerParams(vmem_limit_bytes=60 * 1024 * 1024),
    )(hidden, gain)


def place_kernel(pieces_ref, out_ref):
    for k in range(pieces_ref.shape[0]):
        out_ref[:, 128 * k : 128 * (k + 1)] = pieces_ref[k].astype(f32)


def place_call(pieces, halves):
    count, part, lanes = pieces.shape
    across = count // halves
    return pl.pallas_call(
        place_kernel,
        grid=(halves,),
        in_specs=[pl.BlockSpec((across, part, lanes), lambda i: (i, 0, 0))],
        out_specs=pl.BlockSpec((part, across * lanes), lambda i: (i, 0)),
        out_shape=jax.ShapeDtypeStruct((halves * part, across * lanes), f32),
        compiler_params=pltpu.CompilerParams(vmem_limit_bytes=VMEM_LIMIT),
    )(pieces)


def held_rows(place_ref, own_ref, far_ref, moved_ref):
    x, core = place_ref[0], place_ref[2]
    held = [(2 * x + core, own_ref), (2 * x + 1 - core, far_ref)]
    for j, offset in enumerate(OFFSETS[1:]):
        x_from = lax.rem(x + (offset + 4), 4)
        held += [(2 * x_from + c, moved_ref.at[c, j]) for c in range(2)]
    return held


def margin_kernel(place_ref, tags_ref, delta_ref, columns_ref, own_ref, far_ref, moved_ref, out_ref):
    groups, seq_len, _ = columns_ref.shape
    shape = (2 * groups, seq_len)
    row = lax.broadcasted_iota(jnp.int32, shape, 0)
    lane = lax.broadcasted_iota(jnp.int32, shape, 1)
    me = 2 * place_ref[0] + place_ref[2]
    tags = jnp.where(lane < seq_len // 2, tags_ref[0], tags_ref[1]).astype(f32)
    acc = jnp.where(row == me + groups, tags, 0.0)
    delta = delta_ref[...]
    for seq, read_ref in held_rows(place_ref, own_ref, far_ref, moved_ref):
        value = jnp.dot(columns_ref[seq], delta, preferred_element_type=f32)
        prod = value * read_ref[...].astype(f32)
        part = prod[:, :128]
        for k in range(1, prod.shape[1] // 128):
            part = part + prod[:, 128 * k : 128 * (k + 1)]
        line = jnp.sum(part.T, axis=0, keepdims=True)
        acc = jnp.where(row == seq, line, acc)
    for g in range(out_ref.shape[0]):
        out_ref[g] = acc


def margin_call(place, tags, delta, columns, reads):
    groups, seq_len, _ = columns.shape
    return pl.pallas_call(
        margin_kernel,
        in_specs=[SMEM, SMEM] + [VMEM] * 5,
        out_specs=VMEM,
        out_shape=jax.ShapeDtypeStruct((groups, 2 * groups, seq_len), f32),
        compiler_params=pltpu.CompilerParams(vmem_limit_bytes=VMEM_LIMIT),
    )(place, tags, delta, columns, *reads)


def grad_kernel(
    place_ref, small_ref, columns_ref, own_ref, far_ref, moved_ref, grad_ref, margin_ref, slope_ref
):
    groups, seq_len, share = columns_ref.shape
    small = small_ref[0]
    for g in range(1, groups):
        small = small + small_ref[g]
    label, length = small[groups:, :1], small[groups:, seq_len - 1 :]
    lane = lax.broadcasted_iota(jnp.int32, (groups, seq_len), 1).astype(f32)
    margin = jnp.where(lane < length, small[:groups], 0.0)
    margin_ref[...] = margin
    total = jnp.sum(beta_scale * margin, axis=1, keepdims=True)
    weight = beta_scale * (1.0 / (1.0 + jnp.exp(-total)) - label)
    row = lax.broadcasted_iota(jnp.int32, weight.shape, 0)
    position = lax.broadcasted_iota(jnp.int32, (seq_len, 1), 0).astype(f32)
    for seq, read_ref in held_rows(place_ref, own_ref, far_ref, moved_ref):
        w = jnp.sum(jnp.where(row == seq, weight, 0.0), axis=0, keepdims=True)
        live = position < jnp.sum(jnp.where(row == seq, length, 0.0), axis=0, keepdims=True)
        slope_ref[seq] = (jnp.where(live, w, 0.0) * read_ref[...].astype(f32)).astype(bf16)
    columns = columns_ref[...].reshape(groups * seq_len, share)
    slope = slope_ref[...].reshape(groups * seq_len, slope_ref.shape[2])
    grad = lax.dot_general(
        columns, slope, (((0,), (0,)), ((), ())), preferred_element_type=f32
    ).astype(bf16)
    part = grad_ref.shape[1]
    for yh in range(2):
        for yl in range(2):
            at = (2 * yl + yh) * part
            grad_ref[2 * yh + yl] = grad[at : at + part]


def grad_call(place, small, columns, reads):
    groups, seq_len, share = columns.shape
    features = reads[0].shape[1]
    return pl.pallas_call(
        grad_kernel,
        in_specs=[SMEM] + [VMEM] * 5,
        out_specs=[VMEM, VMEM],
        out_shape=[
            jax.ShapeDtypeStruct((4, share // 4, features), bf16),
            jax.ShapeDtypeStruct((groups, seq_len), f32),
        ],
        scratch_shapes=[pltpu.VMEM((groups, seq_len, features), bf16)],
        compiler_params=pltpu.CompilerParams(vmem_limit_bytes=VMEM_LIMIT),
    )(place, small, columns, *reads)


def shifted(block, axes):
    pairs = [[(i, (i - shift) % 4) for i in range(4)] for shift in OFFSETS[1:]]
    return [block] + [lax.ppermute(block, axes, pair) for pair in pairs]


def on_device(
    hidden, norm_gain, quant_ref, scale_ref, weight_prm, readout, lengths, bounds, labels
):
    seq_len, width = hidden.shape[1:]
    features = readout.shape[2]
    head_size = features // scale_ref.shape[0]
    steps_count = bounds.shape[1]
    group = lax.axis_size(GROUP)
    x, y_lo, core = lax.axis_index("x"), lax.axis_index("yl"), lax.axis_index("c")
    me = 2 * x + core
    place = jnp.stack([x, y_lo, core]).astype(jnp.int32)
    swap = [(0, 1), (1, 0)]
    pieces = norm_call(hidden[0], norm_gain[None], group)
    columns = exchange(pieces, GROUP)
    expanded = jnp.repeat(scale_ref.T, head_size, axis=1)
    ref_local = (quant_ref.astype(f32) * expanded).astype(bf16)
    delta = (weight_prm.astype(f32) - ref_local.astype(f32)).astype(bf16)
    delta_other = lax.ppermute(delta, "yl", swap)
    own, _, _ = lax.optimization_barrier((readout[0], pieces, delta))
    pair = [jnp.where(y_lo == k, delta, delta_other) for k in range(2)]
    delta = jnp.concatenate(pair, axis=0)
    near = shifted(own, ("x",))
    far_own = lax.ppermute(own, "c", swap)
    tags = jnp.concatenate([labels, lengths])
    moved = jnp.stack(near[1:])
    moved, delta, far_own, place, tags = lax.optimization_barrier(
        (moved, delta, far_own, place, tags)
    )
    reads = [own, far_own, lax.all_gather(moved, "c")]
    small = exchange(margin_call(place, tags, delta, columns, reads), GROUP)
    grad, margin = grad_call(place, small, columns, reads)
    grad = wide_sum(exchange(grad, ("yh", "yl"))).astype(bf16)
    zl = lax.axis_size("zl")
    grad = grad.reshape(grad.shape[0], zl, features // zl).transpose(1, 0, 2)
    grad = wide_sum(exchange(grad, ("zl",))).astype(bf16)
    grad = wide_sum(lax.all_gather(grad, "zh")).astype(bf16)
    grad = place_call(spread(grad, ("yh", "zl")), lax.axis_size("yh"))
    position = jnp.arange(seq_len, dtype=jnp.int32)
    reward = beta_scale * lax.dynamic_slice_in_dim(margin, me, 1, axis=0)
    step_index = jnp.sum((position[:, None] >= bounds[0][None, :]).astype(jnp.int32), axis=-1) - 1
    onehot = (step_index[:, None] == jnp.arange(steps_count)[None, :]).astype(f32)
    step_rewards = jnp.sum(reward[0][:, None] * onehot, axis=0)[None]
    return step_rewards, grad


def solution(mesh):
    fine = Mesh(mesh.devices.reshape(2, 4, 4, 2, 4, 2), AXES)
    every = REP + FSDP
    in_specs = (
        P(every, None, None),
        P(),
        P(FSDP, None),
        P(None, FSDP),
        P(FSDP, None),
        P(every, None, None),
        P(every),
        P(every, None),
        P(every),
    )
    out_specs = (P(every, None), P(FSDP, None))
    return jax.shard_map(
        on_device, mesh=fine, in_specs=in_specs, out_specs=out_specs, check_vma=False
    )
```

```python
import jax
import jax.numpy as jnp
from jax import lax
from jax.experimental import pallas as pl
from jax.experimental.pallas import tpu as pltpu
from jax.sharding import Mesh, PartitionSpec as P

epsilon = 1e-06
beta_scale = 0.05

AXES = ("yh", "zh", "zl", "yl", "x", "c")
REP = ("yh", "zh", "zl")
FSDP = ("yl", "x", "c")
GROUP = ("x", "c")
OFFSETS = (0, -1, 1, 2)
VMEM_LIMIT = 24 * 1024 * 1024
VMEM = pl.BlockSpec(memory_space=pltpu.VMEM)
SMEM = pl.BlockSpec(memory_space=pltpu.SMEM)
f32, bf16 = jnp.float32, jnp.bfloat16


def exchange(pieces, axes):
    return lax.all_to_all(pieces, axes, 0, 0, tiled=False)


def spread(block, axes):
    count = lax.axis_size(axes)
    return exchange(jnp.broadcast_to(block[None], (count,) + block.shape), axes)


def wide_sum(parts):
    total = parts[0].astype(f32)
    for k in range(1, parts.shape[0]):
        total = total + parts[k].astype(f32)
    return total


def norm_kernel(hidden_ref, gain_ref, pieces_ref):
    width = hidden_ref.shape[1]
    groups, _, share = pieces_ref.shape
    part = share // 2
    wide = hidden_ref[...].astype(f32)
    mean_square = jnp.sum(wide * wide, axis=-1, keepdims=True) * (1.0 / width)
    scale = lax.rsqrt(mean_square + epsilon)
    normed = (wide * scale * gain_ref[...]).astype(bf16)
    for g in range(groups):
        starts = [(yl * groups + g) * part for yl in range(2)]
        pieces_ref[g] = jnp.concatenate([normed[:, at : at + part] for at in starts], axis=1)


def norm_call(hidden, gain, groups):
    seq_len, width = hidden.shape
    share = width // groups
    block = 64
    return pl.pallas_call(
        norm_kernel,
        grid=(seq_len // block,),
        in_specs=[
            pl.BlockSpec((block, width), lambda i: (i, 0)),
            pl.BlockSpec((1, width), lambda i: (0, 0)),
        ],
        out_specs=pl.BlockSpec((groups, block, share), lambda i: (0, i, 0)),
        out_shape=jax.ShapeDtypeStruct((groups, seq_len, share), bf16),
        compiler_params=pltpu.CompilerParams(vmem_limit_bytes=60 * 1024 * 1024),
    )(hidden, gain)


def place_kernel(sums_ref, pieces_ref, out_ref, steps_ref):
    for k in range(pieces_ref.shape[0]):
        out_ref[:, 128 * k : 128 * (k + 1)] = pieces_ref[k].astype(f32)
    count = steps_ref.shape[1]
    sums = sums_ref[...][:, :count]
    row = lax.broadcasted_iota(jnp.int32, (count, count), 0)
    column = lax.broadcasted_iota(jnp.int32, (count, count), 1)
    steps_ref[...] = jnp.sum(jnp.where(row == column, sums, 0.0), axis=0, keepdims=True)


def place_call(sums, pieces, halves):
    count, part, lanes = pieces.shape
    across = count // halves
    steps = (1, sums.shape[0])
    return pl.pallas_call(
        place_kernel,
        grid=(halves,),
        in_specs=[
            pl.BlockSpec(sums.shape, lambda i: (0, 0)),
            pl.BlockSpec((across, part, lanes), lambda i: (i, 0, 0)),
        ],
        out_specs=[
            pl.BlockSpec((part, across * lanes), lambda i: (i, 0)),
            pl.BlockSpec(steps, lambda i: (0, 0)),
        ],
        out_shape=[
            jax.ShapeDtypeStruct((halves * part, across * lanes), f32),
            jax.ShapeDtypeStruct(steps, f32),
        ],
        compiler_params=pltpu.CompilerParams(vmem_limit_bytes=VMEM_LIMIT),
    )(sums, pieces)


def held_rows(place_ref, own_ref, far_ref, moved_ref):
    x, core = place_ref[0], place_ref[2]
    held = [(2 * x + core, own_ref), (2 * x + 1 - core, far_ref)]
    for j, offset in enumerate(OFFSETS[1:]):
        x_from = lax.rem(x + (offset + 4), 4)
        held += [(2 * x_from + c, moved_ref.at[c, j]) for c in range(2)]
    return held


def margin_kernel(place_ref, tags_ref, delta_ref, columns_ref, own_ref, far_ref, moved_ref, out_ref):
    groups, seq_len, _ = columns_ref.shape
    shape = (2 * groups, seq_len)
    row = lax.broadcasted_iota(jnp.int32, shape, 0)
    lane = lax.broadcasted_iota(jnp.int32, shape, 1)
    me = 2 * place_ref[0] + place_ref[2]
    tags = jnp.where(lane < seq_len // 2, tags_ref[0], tags_ref[1]).astype(f32)
    acc = jnp.where(row == me + groups, tags, 0.0)
    delta = delta_ref[...]
    for seq, read_ref in held_rows(place_ref, own_ref, far_ref, moved_ref):
        value = jnp.dot(columns_ref[seq], delta, preferred_element_type=f32)
        prod = value * read_ref[...].astype(f32)
        part = prod[:, :128]
        for k in range(1, prod.shape[1] // 128):
            part = part + prod[:, 128 * k : 128 * (k + 1)]
        line = jnp.sum(part.T, axis=0, keepdims=True)
        acc = jnp.where(row == seq, line, acc)
    for g in range(out_ref.shape[0]):
        out_ref[g] = acc


def margin_call(place, tags, delta, columns, reads):
    groups, seq_len, _ = columns.shape
    return pl.pallas_call(
        margin_kernel,
        in_specs=[SMEM, SMEM] + [VMEM] * 5,
        out_specs=VMEM,
        out_shape=jax.ShapeDtypeStruct((groups, 2 * groups, seq_len), f32),
        compiler_params=pltpu.CompilerParams(vmem_limit_bytes=VMEM_LIMIT),
    )(place, tags, delta, columns, *reads)


def grad_kernel(
    place_ref, bounds_ref, small_ref, columns_ref, own_ref, far_ref, moved_ref,
    grad_ref, sums_ref, slope_ref
):
    groups, seq_len, share = columns_ref.shape
    small = small_ref[0]
    for g in range(1, groups):
        small = small + small_ref[g]
    label, length = small[groups:, :1], small[groups:, seq_len - 1 :]
    lane = lax.broadcasted_iota(jnp.int32, (groups, seq_len), 1).astype(f32)
    margin = jnp.where(lane < length, small[:groups], 0.0)
    own = lax.broadcasted_iota(jnp.int32, margin.shape, 0) == 2 * place_ref[0] + place_ref[2]
    reward = beta_scale * jnp.sum(jnp.where(own, margin, 0.0), axis=0, keepdims=True)
    steps = bounds_ref.shape[1]
    square = (steps, steps)
    step = lax.broadcasted_iota(jnp.int32, square, 0)
    column = lax.broadcasted_iota(jnp.int32, square, 1)
    first = jnp.broadcast_to(bounds_ref[...].astype(f32), square)
    begin = jnp.sum(jnp.where(column == step, first, 0.0), axis=1, keepdims=True)
    end = jnp.sum(jnp.where(column == step + 1, first, 0.0), axis=1, keepdims=True)
    end = jnp.where(step[:, :1] == steps - 1, float(seq_len), end)
    at = lax.broadcasted_iota(jnp.int32, (steps, seq_len), 1).astype(f32)
    inside = (at >= begin) & (at < end)
    sums = jnp.sum(jnp.where(inside, reward, 0.0), axis=1, keepdims=True)
    sums_ref[...] = jnp.broadcast_to(sums, sums_ref.shape)
    total = jnp.sum(beta_scale * margin, axis=1, keepdims=True)
    weight = beta_scale * (1.0 / (1.0 + jnp.exp(-total)) - label)
    row = lax.broadcasted_iota(jnp.int32, weight.shape, 0)
    position = lax.broadcasted_iota(jnp.int32, (seq_len, 1), 0).astype(f32)
    for seq, read_ref in held_rows(place_ref, own_ref, far_ref, moved_ref):
        w = jnp.sum(jnp.where(row == seq, weight, 0.0), axis=0, keepdims=True)
        live = position < jnp.sum(jnp.where(row == seq, length, 0.0), axis=0, keepdims=True)
        slope_ref[seq] = (jnp.where(live, w, 0.0) * read_ref[...].astype(f32)).astype(bf16)
    columns = columns_ref[...].reshape(groups * seq_len, share)
    slope = slope_ref[...].reshape(groups * seq_len, slope_ref.shape[2])
    grad = lax.dot_general(
        columns, slope, (((0,), (0,)), ((), ())), preferred_element_type=f32
    ).astype(bf16)
    part = grad_ref.shape[1]
    for yh in range(2):
        for yl in range(2):
            at = (2 * yl + yh) * part
            grad_ref[2 * yh + yl] = grad[at : at + part]


def grad_call(place, bounds, small, columns, reads):
    groups, seq_len, share = columns.shape
    features = reads[0].shape[1]
    return pl.pallas_call(
        grad_kernel,
        in_specs=[SMEM] + [VMEM] * 6,
        out_specs=[VMEM, VMEM],
        out_shape=[
            jax.ShapeDtypeStruct((4, share // 4, features), bf16),
            jax.ShapeDtypeStruct((bounds.shape[1], seq_len), f32),
        ],
        scratch_shapes=[pltpu.VMEM((groups, seq_len, features), bf16)],
        compiler_params=pltpu.CompilerParams(vmem_limit_bytes=VMEM_LIMIT),
    )(place, bounds, small, columns, *reads)


def shifted(block, axes):
    pairs = [[(i, (i - shift) % 4) for i in range(4)] for shift in OFFSETS[1:]]
    return [block] + [lax.ppermute(block, axes, pair) for pair in pairs]


def on_device(
    hidden, norm_gain, quant_ref, scale_ref, weight_prm, readout, lengths, bounds, labels
):
    seq_len, width = hidden.shape[1:]
    features = readout.shape[2]
    head_size = features // scale_ref.shape[0]
    group = lax.axis_size(GROUP)
    x, y_lo, core = lax.axis_index("x"), lax.axis_index("yl"), lax.axis_index("c")
    place = jnp.stack([x, y_lo, core]).astype(jnp.int32)
    swap = [(0, 1), (1, 0)]
    pieces = norm_call(hidden[0], norm_gain[None], group)
    columns = exchange(pieces, GROUP)
    expanded = jnp.repeat(scale_ref.T, head_size, axis=1)
    ref_local = (quant_ref.astype(f32) * expanded).astype(bf16)
    delta = (weight_prm.astype(f32) - ref_local.astype(f32)).astype(bf16)
    delta_other = lax.ppermute(delta, "yl", swap)
    own, _, _ = lax.optimization_barrier((readout[0], pieces, delta))
    pair = [jnp.where(y_lo == k, delta, delta_other) for k in range(2)]
    delta = jnp.concatenate(pair, axis=0)
    near = shifted(own, ("x",))
    far_own = lax.ppermute(own, "c", swap)
    tags = jnp.concatenate([labels, lengths])
    moved = jnp.stack(near[1:])
    moved, delta, far_own, place, tags = lax.optimization_barrier(
        (moved, delta, far_own, place, tags)
    )
    reads = [own, far_own, lax.all_gather(moved, "c")]
    small = exchange(margin_call(place, tags, delta, columns, reads), GROUP)
    grad, sums = grad_call(place, bounds, small, columns, reads)
    grad = wide_sum(exchange(grad, ("yh", "yl"))).astype(bf16)
    zl = lax.axis_size("zl")
    grad = grad.reshape(grad.shape[0], zl, features // zl).transpose(1, 0, 2)
    grad = wide_sum(exchange(grad, ("zl",))).astype(bf16)
    grad = wide_sum(lax.all_gather(grad, "zh")).astype(bf16)
    grad = spread(grad, ("yh", "zl"))
    grad, step_rewards = place_call(sums, grad, lax.axis_size("yh"))
    return step_rewards, grad


def solution(mesh):
    fine = Mesh(mesh.devices.reshape(2, 4, 4, 2, 4, 2), AXES)
    every = REP + FSDP
    in_specs = (
        P(every, None, None),
        P(),
        P(FSDP, None),
        P(None, FSDP),
        P(FSDP, None),
        P(every, None, None),
        P(every),
        P(every, None),
        P(every),
    )
    out_specs = (P(every, None), P(FSDP, None))
    return jax.shard_map(
        on_device, mesh=fine, in_specs=in_specs, out_specs=out_specs, check_vma=False
    )
```

```python
import jax
import jax.numpy as jnp
from jax import lax
from jax.experimental import pallas as pl
from jax.experimental.pallas import tpu as pltpu
from jax.sharding import Mesh, PartitionSpec as P

epsilon = 1e-06
beta_scale = 0.05

AXES = ("yh", "zh", "zl", "yl", "x", "c")
REP = ("yh", "zh", "zl")
FSDP = ("yl", "x", "c")
GROUP = ("x", "c")
OFFSETS = (0, -1, 1, 2)
VMEM_LIMIT = 24 * 1024 * 1024
VMEM = pl.BlockSpec(memory_space=pltpu.VMEM)
SMEM = pl.BlockSpec(memory_space=pltpu.SMEM)
f32, bf16 = jnp.float32, jnp.bfloat16


def exchange(pieces, axes):
    return lax.all_to_all(pieces, axes, 0, 0, tiled=False)


def spread(block, axes):
    count = lax.axis_size(axes)
    return exchange(jnp.broadcast_to(block[None], (count,) + block.shape), axes)


def wide_sum(parts):
    total = parts[0].astype(f32)
    for k in range(1, parts.shape[0]):
        total = total + parts[k].astype(f32)
    return total


def norm_kernel(hidden_ref, gain_ref, pieces_ref):
    width = hidden_ref.shape[1]
    groups, _, share = pieces_ref.shape
    part = share // 2
    wide = hidden_ref[...].astype(f32)
    mean_square = jnp.sum(wide * wide, axis=-1, keepdims=True) * (1.0 / width)
    scale = lax.rsqrt(mean_square + epsilon)
    normed = (wide * scale * gain_ref[...]).astype(bf16)
    for g in range(groups):
        starts = [(yl * groups + g) * part for yl in range(2)]
        pieces_ref[g] = jnp.concatenate([normed[:, at : at + part] for at in starts], axis=1)


def norm_call(hidden, gain, groups):
    seq_len, width = hidden.shape
    share = width // groups
    block = 64
    return pl.pallas_call(
        norm_kernel,
        grid=(seq_len // block,),
        in_specs=[
            pl.BlockSpec((block, width), lambda i: (i, 0)),
            pl.BlockSpec((1, width), lambda i: (0, 0)),
        ],
        out_specs=pl.BlockSpec((groups, block, share), lambda i: (0, i, 0)),
        out_shape=jax.ShapeDtypeStruct((groups, seq_len, share), bf16),
        compiler_params=pltpu.CompilerParams(vmem_limit_bytes=60 * 1024 * 1024),
    )(hidden, gain)


def place_kernel(sums_ref, pieces_ref, out_ref, steps_ref):
    for k in range(pieces_ref.shape[0]):
        out_ref[:, 128 * k : 128 * (k + 1)] = pieces_ref[k].astype(f32)
    count = steps_ref.shape[1]
    sums = sums_ref[...][:, :count]
    row = lax.broadcasted_iota(jnp.int32, (count, count), 0)
    column = lax.broadcasted_iota(jnp.int32, (count, count), 1)
    steps_ref[...] = jnp.sum(jnp.where(row == column, sums, 0.0), axis=0, keepdims=True)


def place_call(sums, pieces, halves):
    count, part, lanes = pieces.shape
    across = count // halves
    steps = (1, sums.shape[0])
    return pl.pallas_call(
        place_kernel,
        grid=(halves,),
        in_specs=[
            pl.BlockSpec(sums.shape, lambda i: (0, 0)),
            pl.BlockSpec((across, part, lanes), lambda i: (i, 0, 0)),
        ],
        out_specs=[
            pl.BlockSpec((part, across * lanes), lambda i: (i, 0)),
            pl.BlockSpec(steps, lambda i: (0, 0)),
        ],
        out_shape=[
            jax.ShapeDtypeStruct((halves * part, across * lanes), f32),
            jax.ShapeDtypeStruct(steps, f32),
        ],
        compiler_params=pltpu.CompilerParams(vmem_limit_bytes=VMEM_LIMIT),
    )(sums, pieces)


def held_rows(place_ref, own_ref, far_ref, moved_ref, across_ref):
    x, core = place_ref[0], place_ref[2]
    held = [(2 * x + core, own_ref), (2 * x + 1 - core, far_ref)]
    for j, offset in enumerate(OFFSETS[1:]):
        x_from = lax.rem(x + (offset + 4), 4)
        refs = [across_ref.at[c] if offset == 2 else moved_ref.at[c, j] for c in range(2)]
        held += [(2 * x_from + c, refs[c]) for c in range(2)]
    return held


def margin_kernel(
    place_ref, tags_ref, delta_ref, columns_ref, own_ref, far_ref, moved_ref, across_ref, out_ref
):
    groups, seq_len, _ = columns_ref.shape
    shape = (2 * groups, seq_len)
    row = lax.broadcasted_iota(jnp.int32, shape, 0)
    lane = lax.broadcasted_iota(jnp.int32, shape, 1)
    me = 2 * place_ref[0] + place_ref[2]
    tags = jnp.where(lane < seq_len // 2, tags_ref[0], tags_ref[1]).astype(f32)
    acc = jnp.where(row == me + groups, tags, 0.0)
    delta = delta_ref[...]
    for seq, read_ref in held_rows(place_ref, own_ref, far_ref, moved_ref, across_ref):
        value = jnp.dot(columns_ref[seq], delta, preferred_element_type=f32)
        prod = value * read_ref[...].astype(f32)
        part = prod[:, :128]
        for k in range(1, prod.shape[1] // 128):
            part = part + prod[:, 128 * k : 128 * (k + 1)]
        line = jnp.sum(part.T, axis=0, keepdims=True)
        acc = jnp.where(row == seq, line, acc)
    for g in range(out_ref.shape[0]):
        out_ref[g] = acc


def margin_call(place, tags, delta, columns, reads):
    groups, seq_len, _ = columns.shape
    return pl.pallas_call(
        margin_kernel,
        in_specs=[SMEM, SMEM] + [VMEM] * 6,
        out_specs=VMEM,
        out_shape=jax.ShapeDtypeStruct((groups, 2 * groups, seq_len), f32),
        compiler_params=pltpu.CompilerParams(vmem_limit_bytes=VMEM_LIMIT),
    )(place, tags, delta, columns, *reads)


def grad_kernel(
    place_ref, bounds_ref, small_ref, columns_ref, own_ref, far_ref, moved_ref, across_ref,
    grad_ref, sums_ref, slope_ref
):
    groups, seq_len, share = columns_ref.shape
    small = small_ref[0]
    for g in range(1, groups):
        small = small + small_ref[g]
    label, length = small[groups:, :1], small[groups:, seq_len - 1 :]
    lane = lax.broadcasted_iota(jnp.int32, (groups, seq_len), 1).astype(f32)
    margin = jnp.where(lane < length, small[:groups], 0.0)
    own = lax.broadcasted_iota(jnp.int32, margin.shape, 0) == 2 * place_ref[0] + place_ref[2]
    reward = beta_scale * jnp.sum(jnp.where(own, margin, 0.0), axis=0, keepdims=True)
    steps = bounds_ref.shape[1]
    square = (steps, steps)
    step = lax.broadcasted_iota(jnp.int32, square, 0)
    column = lax.broadcasted_iota(jnp.int32, square, 1)
    first = jnp.broadcast_to(bounds_ref[...].astype(f32), square)
    begin = jnp.sum(jnp.where(column == step, first, 0.0), axis=1, keepdims=True)
    end = jnp.sum(jnp.where(column == step + 1, first, 0.0), axis=1, keepdims=True)
    end = jnp.where(step[:, :1] == steps - 1, float(seq_len), end)
    at = lax.broadcasted_iota(jnp.int32, (steps, seq_len), 1).astype(f32)
    inside = (at >= begin) & (at < end)
    sums = jnp.sum(jnp.where(inside, reward, 0.0), axis=1, keepdims=True)
    sums_ref[...] = jnp.broadcast_to(sums, sums_ref.shape)
    total = jnp.sum(beta_scale * margin, axis=1, keepdims=True)
    weight = beta_scale * (1.0 / (1.0 + jnp.exp(-total)) - label)
    row = lax.broadcasted_iota(jnp.int32, weight.shape, 0)
    position = lax.broadcasted_iota(jnp.int32, (seq_len, 1), 0).astype(f32)
    for seq, read_ref in held_rows(place_ref, own_ref, far_ref, moved_ref, across_ref):
        w = jnp.sum(jnp.where(row == seq, weight, 0.0), axis=0, keepdims=True)
        live = position < jnp.sum(jnp.where(row == seq, length, 0.0), axis=0, keepdims=True)
        slope_ref[seq] = (jnp.where(live, w, 0.0) * read_ref[...].astype(f32)).astype(bf16)
    columns = columns_ref[...].reshape(groups * seq_len, share)
    slope = slope_ref[...].reshape(groups * seq_len, slope_ref.shape[2])
    grad = lax.dot_general(
        columns, slope, (((0,), (0,)), ((), ())), preferred_element_type=f32
    ).astype(bf16)
    part = grad_ref.shape[1]
    for yh in range(2):
        for yl in range(2):
            at = (2 * yl + yh) * part
            grad_ref[2 * yh + yl] = grad[at : at + part]


def grad_call(place, bounds, small, columns, reads):
    groups, seq_len, share = columns.shape
    features = reads[0].shape[1]
    return pl.pallas_call(
        grad_kernel,
        in_specs=[SMEM] + [VMEM] * 7,
        out_specs=[VMEM, VMEM],
        out_shape=[
            jax.ShapeDtypeStruct((4, share // 4, features), bf16),
            jax.ShapeDtypeStruct((bounds.shape[1], seq_len), f32),
        ],
        scratch_shapes=[pltpu.VMEM((groups, seq_len, features), bf16)],
        compiler_params=pltpu.CompilerParams(vmem_limit_bytes=VMEM_LIMIT),
    )(place, bounds, small, columns, *reads)


def shifted(block, axes):
    pairs = [[(i, (i - shift) % 4) for i in range(4)] for shift in OFFSETS[1:]]
    return [block] + [lax.ppermute(block, axes, pair) for pair in pairs]


def on_device(
    hidden, norm_gain, quant_ref, scale_ref, weight_prm, readout, lengths, bounds, labels
):
    seq_len, width = hidden.shape[1:]
    features = readout.shape[2]
    head_size = features // scale_ref.shape[0]
    group = lax.axis_size(GROUP)
    x, y_lo, core = lax.axis_index("x"), lax.axis_index("yl"), lax.axis_index("c")
    place = jnp.stack([x, y_lo, core]).astype(jnp.int32)
    swap = [(0, 1), (1, 0)]
    pieces = norm_call(hidden[0], norm_gain[None], group)
    columns = exchange(pieces, GROUP)
    weight_prm, _ = lax.optimization_barrier((weight_prm, pieces))
    expanded = jnp.repeat(scale_ref.T, head_size, axis=1)
    ref_local = (quant_ref.astype(f32) * expanded).astype(bf16)
    delta = (weight_prm.astype(f32) - ref_local.astype(f32)).astype(bf16)
    delta_other = lax.ppermute(delta, "yl", swap)
    own, _, _ = lax.optimization_barrier((readout[0], pieces, delta))
    pair = [jnp.where(y_lo == k, delta, delta_other) for k in range(2)]
    delta = jnp.concatenate(pair, axis=0)
    near = shifted(own, ("x",))
    late, _ = lax.optimization_barrier((own, delta))
    far_own = lax.ppermute(late, "c", swap)
    tags = jnp.concatenate([labels, lengths])
    across = lax.all_gather(near[3], "c")
    moved = jnp.stack(near[1:3])
    moved, across, delta, far_own, place, tags = lax.optimization_barrier(
        (moved, across, delta, far_own, place, tags)
    )
    reads = [own, far_own, lax.all_gather(moved, "c"), across]
    small = exchange(margin_call(place, tags, delta, columns, reads), GROUP)
    grad, sums = grad_call(place, bounds, small, columns, reads)
    grad = wide_sum(exchange(grad, ("yh", "yl"))).astype(bf16)
    zl = lax.axis_size("zl")
    grad = grad.reshape(grad.shape[0], zl, features // zl).transpose(1, 0, 2)
    grad = wide_sum(exchange(grad, ("zl",))).astype(bf16)
    grad = wide_sum(lax.all_gather(grad, "zh")).astype(bf16)
    grad = spread(grad, ("yh", "zl"))
    grad, step_rewards = place_call(sums, grad, lax.axis_size("yh"))
    return step_rewards, grad


def solution(mesh):
    fine = Mesh(mesh.devices.reshape(2, 4, 4, 2, 4, 2), AXES)
    every = REP + FSDP
    in_specs = (
        P(every, None, None),
        P(),
        P(FSDP, None),
        P(None, FSDP),
        P(FSDP, None),
        P(every, None, None),
        P(every),
        P(every, None),
        P(every),
    )
    out_specs = (P(every, None), P(FSDP, None))
    return jax.shard_map(
        on_device, mesh=fine, in_specs=in_specs, out_specs=out_specs, check_vma=False
    )
```

```python
import jax
import jax.numpy as jnp
from jax import lax
from jax.experimental import pallas as pl
from jax.experimental.pallas import tpu as pltpu
from jax.sharding import Mesh, PartitionSpec as P

epsilon = 1e-06
beta_scale = 0.05

AXES = ("yh", "zh", "zl", "yl", "x", "c")
REP = ("yh", "zh", "zl")
FSDP = ("yl", "x", "c")
GROUP = ("x", "c")
OFFSETS = (0, -1, 1, 2)
VMEM_LIMIT = 24 * 1024 * 1024
VMEM = pl.BlockSpec(memory_space=pltpu.VMEM)
SMEM = pl.BlockSpec(memory_space=pltpu.SMEM)
f32, bf16 = jnp.float32, jnp.bfloat16


def exchange(pieces, axes):
    return lax.all_to_all(pieces, axes, 0, 0, tiled=False)


def spread(block, axes):
    count = lax.axis_size(axes)
    return exchange(jnp.broadcast_to(block[None], (count,) + block.shape), axes)


def wide_sum(parts):
    total = parts[0].astype(f32)
    for k in range(1, parts.shape[0]):
        total = total + parts[k].astype(f32)
    return total


def norm_kernel(hidden_ref, gain_ref, pieces_ref):
    width = hidden_ref.shape[1]
    groups, _, share = pieces_ref.shape
    part = share // 2
    wide = hidden_ref[...].astype(f32)
    mean_square = jnp.sum(wide * wide, axis=-1, keepdims=True) * (1.0 / width)
    scale = lax.rsqrt(mean_square + epsilon)
    normed = (wide * scale * gain_ref[...]).astype(bf16)
    for g in range(groups):
        starts = [(yl * groups + g) * part for yl in range(2)]
        pieces_ref[g] = jnp.concatenate([normed[:, at : at + part] for at in starts], axis=1)


def norm_call(hidden, gain, groups):
    seq_len, width = hidden.shape
    share = width // groups
    block = 64
    return pl.pallas_call(
        norm_kernel,
        grid=(seq_len // block,),
        in_specs=[
            pl.BlockSpec((block, width), lambda i: (i, 0)),
            pl.BlockSpec((1, width), lambda i: (0, 0)),
        ],
        out_specs=pl.BlockSpec((groups, block, share), lambda i: (0, i, 0)),
        out_shape=jax.ShapeDtypeStruct((groups, seq_len, share), bf16),
        compiler_params=pltpu.CompilerParams(vmem_limit_bytes=60 * 1024 * 1024),
    )(hidden, gain)


def place_kernel(sums_ref, pieces_ref, out_ref, steps_ref):
    for k in range(pieces_ref.shape[0]):
        out_ref[:, 128 * k : 128 * (k + 1)] = pieces_ref[k].astype(f32)
    count = steps_ref.shape[1]
    sums = sums_ref[...][:, :count]
    row = lax.broadcasted_iota(jnp.int32, (count, count), 0)
    column = lax.broadcasted_iota(jnp.int32, (count, count), 1)
    steps_ref[...] = jnp.sum(jnp.where(row == column, sums, 0.0), axis=0, keepdims=True)


def place_call(sums, pieces, halves):
    count, part, lanes = pieces.shape
    across = count // halves
    steps = (1, sums.shape[0])
    return pl.pallas_call(
        place_kernel,
        grid=(halves,),
        in_specs=[
            pl.BlockSpec(sums.shape, lambda i: (0, 0)),
            pl.BlockSpec((across, part, lanes), lambda i: (i, 0, 0)),
        ],
        out_specs=[
            pl.BlockSpec((part, across * lanes), lambda i: (i, 0)),
            pl.BlockSpec(steps, lambda i: (0, 0)),
        ],
        out_shape=[
            jax.ShapeDtypeStruct((halves * part, across * lanes), f32),
            jax.ShapeDtypeStruct(steps, f32),
        ],
        compiler_params=pltpu.CompilerParams(vmem_limit_bytes=VMEM_LIMIT),
    )(sums, pieces)


def held_rows(place_ref, own_ref, far_ref, moved_ref, across_ref):
    x, core = place_ref[0], place_ref[2]
    held = [(2 * x + core, own_ref), (2 * x + 1 - core, far_ref)]
    for j, offset in enumerate(OFFSETS[1:]):
        x_from = lax.rem(x + (offset + 4), 4)
        refs = [across_ref.at[c] if offset == 2 else moved_ref.at[c, j] for c in range(2)]
        held += [(2 * x_from + c, refs[c]) for c in range(2)]
    return held


def margin_kernel(
    place_ref, tags_ref, delta_ref, columns_ref, own_ref, far_ref, moved_ref, across_ref, out_ref
):
    groups, seq_len, _ = columns_ref.shape
    shape = (2 * groups, seq_len)
    row = lax.broadcasted_iota(jnp.int32, shape, 0)
    lane = lax.broadcasted_iota(jnp.int32, shape, 1)
    me = 2 * place_ref[0] + place_ref[2]
    tags = jnp.where(lane < seq_len // 2, tags_ref[0], tags_ref[1]).astype(f32)
    acc = jnp.where(row == me + groups, tags, 0.0)
    delta = delta_ref[...]
    for seq, read_ref in held_rows(place_ref, own_ref, far_ref, moved_ref, across_ref):
        value = jnp.dot(columns_ref[seq], delta, preferred_element_type=f32)
        prod = value * read_ref[...].astype(f32)
        part = prod[:, :128]
        for k in range(1, prod.shape[1] // 128):
            part = part + prod[:, 128 * k : 128 * (k + 1)]
        line = jnp.sum(part.T, axis=0, keepdims=True)
        acc = jnp.where(row == seq, line, acc)
    for g in range(out_ref.shape[0]):
        out_ref[g] = acc


def margin_call(place, tags, delta, columns, reads):
    groups, seq_len, _ = columns.shape
    return pl.pallas_call(
        margin_kernel,
        in_specs=[SMEM, SMEM] + [VMEM] * 6,
        out_specs=VMEM,
        out_shape=jax.ShapeDtypeStruct((groups, 2 * groups, seq_len), f32),
        compiler_params=pltpu.CompilerParams(vmem_limit_bytes=VMEM_LIMIT),
    )(place, tags, delta, columns, *reads)


def grad_kernel(
    place_ref, bounds_ref, small_ref, columns_ref, own_ref, far_ref, moved_ref, across_ref,
    grad_ref, sums_ref, slope_ref
):
    groups, seq_len, share = columns_ref.shape
    small = small_ref[0]
    for g in range(1, groups):
        small = small + small_ref[g]
    label, length = small[groups:, :1], small[groups:, seq_len - 1 :]
    lane = lax.broadcasted_iota(jnp.int32, (groups, seq_len), 1).astype(f32)
    margin = jnp.where(lane < length, small[:groups], 0.0)
    own = lax.broadcasted_iota(jnp.int32, margin.shape, 0) == 2 * place_ref[0] + place_ref[2]
    reward = beta_scale * jnp.sum(jnp.where(own, margin, 0.0), axis=0, keepdims=True)
    steps = bounds_ref.shape[1]
    square = (steps, steps)
    step = lax.broadcasted_iota(jnp.int32, square, 0)
    column = lax.broadcasted_iota(jnp.int32, square, 1)
    first = jnp.broadcast_to(bounds_ref[...].astype(f32), square)
    begin = jnp.sum(jnp.where(column == step, first, 0.0), axis=1, keepdims=True)
    end = jnp.sum(jnp.where(column == step + 1, first, 0.0), axis=1, keepdims=True)
    end = jnp.where(step[:, :1] == steps - 1, float(seq_len), end)
    at = lax.broadcasted_iota(jnp.int32, (steps, seq_len), 1).astype(f32)
    inside = (at >= begin) & (at < end)
    sums = jnp.sum(jnp.where(inside, reward, 0.0), axis=1, keepdims=True)
    sums_ref[...] = jnp.broadcast_to(sums, sums_ref.shape)
    total = jnp.sum(beta_scale * margin, axis=1, keepdims=True)
    weight = beta_scale * (1.0 / (1.0 + jnp.exp(-total)) - label)
    row = lax.broadcasted_iota(jnp.int32, weight.shape, 0)
    position = lax.broadcasted_iota(jnp.int32, (seq_len, 1), 0).astype(f32)
    for seq, read_ref in held_rows(place_ref, own_ref, far_ref, moved_ref, across_ref):
        w = jnp.sum(jnp.where(row == seq, weight, 0.0), axis=0, keepdims=True)
        live = position < jnp.sum(jnp.where(row == seq, length, 0.0), axis=0, keepdims=True)
        slope_ref[seq] = (jnp.where(live, w, 0.0) * read_ref[...].astype(f32)).astype(bf16)
    columns = columns_ref[...].reshape(groups * seq_len, share)
    slope = slope_ref[...].reshape(groups * seq_len, slope_ref.shape[2])
    grad = lax.dot_general(
        columns, slope, (((0,), (0,)), ((), ())), preferred_element_type=f32
    ).astype(bf16)
    part = grad_ref.shape[1]
    for yh in range(2):
        for yl in range(2):
            at = (2 * yl + yh) * part
            for zl in range(4):
                piece = grad[at : at + part, 128 * zl : 128 * (zl + 1)]
                grad_ref[8 * yh + 4 * yl + zl] = piece


def grad_call(place, bounds, small, columns, reads):
    groups, seq_len, share = columns.shape
    features = reads[0].shape[1]
    return pl.pallas_call(
        grad_kernel,
        in_specs=[SMEM] + [VMEM] * 7,
        out_specs=[VMEM, VMEM],
        out_shape=[
            jax.ShapeDtypeStruct((16, share // 4, features // 4), bf16),
            jax.ShapeDtypeStruct((bounds.shape[1], seq_len), f32),
        ],
        scratch_shapes=[pltpu.VMEM((groups, seq_len, features), bf16)],
        compiler_params=pltpu.CompilerParams(vmem_limit_bytes=VMEM_LIMIT),
    )(place, bounds, small, columns, *reads)


def shifted(block, axes):
    pairs = [[(i, (i - shift) % 4) for i in range(4)] for shift in OFFSETS[1:]]
    return [block] + [lax.ppermute(block, axes, pair) for pair in pairs]


def on_device(
    hidden, norm_gain, quant_ref, scale_ref, weight_prm, readout, lengths, bounds, labels
):
    seq_len, width = hidden.shape[1:]
    features = readout.shape[2]
    head_size = features // scale_ref.shape[0]
    group = lax.axis_size(GROUP)
    x, y_lo, core = lax.axis_index("x"), lax.axis_index("yl"), lax.axis_index("c")
    place = jnp.stack([x, y_lo, core]).astype(jnp.int32)
    swap = [(0, 1), (1, 0)]
    pieces = norm_call(hidden[0], norm_gain[None], group)
    columns = exchange(pieces, GROUP)
    weight_prm, _ = lax.optimization_barrier((weight_prm, pieces))
    expanded = jnp.repeat(scale_ref.T, head_size, axis=1)
    ref_local = (quant_ref.astype(f32) * expanded).astype(bf16)
    delta = (weight_prm.astype(f32) - ref_local.astype(f32)).astype(bf16)
    delta_other = lax.ppermute(delta, "yl", swap)
    own, _, _ = lax.optimization_barrier((readout[0], pieces, delta))
    pair = [jnp.where(y_lo == k, delta, delta_other) for k in range(2)]
    delta = jnp.concatenate(pair, axis=0)
    near = shifted(own, ("x",))
    late, _ = lax.optimization_barrier((own, delta))
    far_own = lax.ppermute(late, "c", swap)
    tags = jnp.concatenate([labels, lengths])
    across = lax.all_gather(near[3], "c")
    moved = jnp.stack(near[1:3])
    moved, across, delta, far_own, place, tags = lax.optimization_barrier(
        (moved, across, delta, far_own, place, tags)
    )
    reads = [own, far_own, lax.all_gather(moved, "c"), across]
    small = exchange(margin_call(place, tags, delta, columns, reads), GROUP)
    grad, sums = grad_call(place, bounds, small, columns, reads)
    grad = wide_sum(exchange(grad, ("yh", "yl", "zl"))).astype(bf16)
    grad = wide_sum(lax.all_gather(grad, "zh")).astype(bf16)
    grad = spread(grad, ("yh", "zl"))
    grad, step_rewards = place_call(sums, grad, lax.axis_size("yh"))
    return step_rewards, grad


def solution(mesh):
    fine = Mesh(mesh.devices.reshape(2, 4, 4, 2, 4, 2), AXES)
    every = REP + FSDP
    in_specs = (
        P(every, None, None),
        P(),
        P(FSDP, None),
        P(None, FSDP),
        P(FSDP, None),
        P(every, None, None),
        P(every),
        P(every, None),
        P(every),
    )
    out_specs = (P(every, None), P(FSDP, None))
    return jax.shard_map(
        on_device, mesh=fine, in_specs=in_specs, out_specs=out_specs, check_vma=False
    )
```

```python
import jax
import jax.numpy as jnp
from jax import lax
from jax.experimental import pallas as pl
from jax.experimental.pallas import tpu as pltpu
from jax.sharding import Mesh, PartitionSpec as P

epsilon = 1e-06
beta_scale = 0.05

AXES = ("yh", "zh", "zl", "yl", "x", "c")
REP = ("yh", "zh", "zl")
FSDP = ("yl", "x", "c")
GROUP = ("x", "c")
OFFSETS = (0, -1, 1, 2)
VMEM_LIMIT = 24 * 1024 * 1024
VMEM = pl.BlockSpec(memory_space=pltpu.VMEM)
SMEM = pl.BlockSpec(memory_space=pltpu.SMEM)
f32, bf16 = jnp.float32, jnp.bfloat16


def exchange(pieces, axes):
    return lax.all_to_all(pieces, axes, 0, 0, tiled=False)


def spread(block, axes):
    count = lax.axis_size(axes)
    return exchange(jnp.broadcast_to(block[None], (count,) + block.shape), axes)


def wide_sum(parts):
    total = parts[0].astype(f32)
    for k in range(1, parts.shape[0]):
        total = total + parts[k].astype(f32)
    return total


def norm_kernel(hidden_ref, gain_ref, pieces_ref):
    width = hidden_ref.shape[1]
    groups, _, share = pieces_ref.shape
    part = share // 2
    wide = hidden_ref[...].astype(f32)
    mean_square = jnp.sum(wide * wide, axis=-1, keepdims=True) * (1.0 / width)
    scale = lax.rsqrt(mean_square + epsilon)
    normed = (wide * scale * gain_ref[...]).astype(bf16)
    for g in range(groups):
        starts = [(yl * groups + g) * part for yl in range(2)]
        pieces_ref[g] = jnp.concatenate([normed[:, at : at + part] for at in starts], axis=1)


def norm_call(hidden, gain, groups):
    seq_len, width = hidden.shape
    share = width // groups
    block = 64
    return pl.pallas_call(
        norm_kernel,
        grid=(seq_len // block,),
        in_specs=[
            pl.BlockSpec((block, width), lambda i: (i, 0)),
            pl.BlockSpec((1, width), lambda i: (0, 0)),
        ],
        out_specs=pl.BlockSpec((groups, block, share), lambda i: (0, i, 0)),
        out_shape=jax.ShapeDtypeStruct((groups, seq_len, share), bf16),
        compiler_params=pltpu.CompilerParams(vmem_limit_bytes=60 * 1024 * 1024),
    )(hidden, gain)


def place_kernel(sums_ref, pieces_ref, out_ref, steps_ref):
    for k in range(pieces_ref.shape[0]):
        out_ref[:, 128 * k : 128 * (k + 1)] = pieces_ref[k].astype(f32)
    count = steps_ref.shape[1]
    sums = sums_ref[...][:, :count]
    row = lax.broadcasted_iota(jnp.int32, (count, count), 0)
    column = lax.broadcasted_iota(jnp.int32, (count, count), 1)
    steps_ref[...] = jnp.sum(jnp.where(row == column, sums, 0.0), axis=0, keepdims=True)


def place_call(sums, pieces, halves):
    count, part, lanes = pieces.shape
    across = count // halves
    steps = (1, sums.shape[0])
    return pl.pallas_call(
        place_kernel,
        grid=(halves,),
        in_specs=[
            pl.BlockSpec(sums.shape, lambda i: (0, 0)),
            pl.BlockSpec((across, part, lanes), lambda i: (i, 0, 0)),
        ],
        out_specs=[
            pl.BlockSpec((part, across * lanes), lambda i: (i, 0)),
            pl.BlockSpec(steps, lambda i: (0, 0)),
        ],
        out_shape=[
            jax.ShapeDtypeStruct((halves * part, across * lanes), f32),
            jax.ShapeDtypeStruct(steps, f32),
        ],
        compiler_params=pltpu.CompilerParams(vmem_limit_bytes=VMEM_LIMIT),
    )(sums, pieces)


def held_rows(place_ref, own_ref, far_ref, moved_ref, across_ref):
    x, core = place_ref[0], place_ref[2]
    held = [(2 * x + core, own_ref), (2 * x + 1 - core, far_ref)]
    for j, offset in enumerate(OFFSETS[1:]):
        x_from = lax.rem(x + (offset + 4), 4)
        refs = [across_ref.at[c] if offset == 2 else moved_ref.at[c, j] for c in range(2)]
        held += [(2 * x_from + c, refs[c]) for c in range(2)]
    return held


def margin_kernel(
    place_ref, tags_ref, delta_ref, columns_ref, own_ref, far_ref, moved_ref, across_ref, out_ref
):
    groups, seq_len, _ = columns_ref.shape
    shape = (2 * groups, seq_len)
    row = lax.broadcasted_iota(jnp.int32, shape, 0)
    lane = lax.broadcasted_iota(jnp.int32, shape, 1)
    me = 2 * place_ref[0] + place_ref[2]
    tags = jnp.where(lane < seq_len // 2, tags_ref[0], tags_ref[1]).astype(f32)
    acc = jnp.where(row == me + groups, tags, 0.0)
    delta = delta_ref[...]
    for seq, read_ref in held_rows(place_ref, own_ref, far_ref, moved_ref, across_ref):
        value = jnp.dot(columns_ref[seq], delta, preferred_element_type=f32)
        prod = value * read_ref[...].astype(f32)
        part = prod[:, :128]
        for k in range(1, prod.shape[1] // 128):
            part = part + prod[:, 128 * k : 128 * (k + 1)]
        line = jnp.sum(part.T, axis=0, keepdims=True)
        acc = jnp.where(row == seq, line, acc)
    for g in range(out_ref.shape[0]):
        out_ref[g] = acc


def margin_call(place, tags, delta, columns, reads):
    groups, seq_len, _ = columns.shape
    return pl.pallas_call(
        margin_kernel,
        in_specs=[SMEM, SMEM] + [VMEM] * 6,
        out_specs=VMEM,
        out_shape=jax.ShapeDtypeStruct((groups, 2 * groups, seq_len), f32),
        compiler_params=pltpu.CompilerParams(vmem_limit_bytes=VMEM_LIMIT),
    )(place, tags, delta, columns, *reads)


def grad_kernel(
    place_ref, bounds_ref, small_ref, columns_ref, own_ref, far_ref, moved_ref, across_ref,
    grad_ref, sums_ref, slope_ref
):
    groups, seq_len, share = columns_ref.shape
    small = small_ref[0]
    for g in range(1, groups):
        small = small + small_ref[g]
    label, length = small[groups:, :1], small[groups:, seq_len - 1 :]
    lane = lax.broadcasted_iota(jnp.int32, (groups, seq_len), 1).astype(f32)
    margin = jnp.where(lane < length, small[:groups], 0.0)
    own = lax.broadcasted_iota(jnp.int32, margin.shape, 0) == 2 * place_ref[0] + place_ref[2]
    reward = beta_scale * jnp.sum(jnp.where(own, margin, 0.0), axis=0, keepdims=True)
    steps = bounds_ref.shape[1]
    square = (steps, steps)
    step = lax.broadcasted_iota(jnp.int32, square, 0)
    column = lax.broadcasted_iota(jnp.int32, square, 1)
    first = jnp.broadcast_to(bounds_ref[...].astype(f32), square)
    begin = jnp.sum(jnp.where(column == step, first, 0.0), axis=1, keepdims=True)
    end = jnp.sum(jnp.where(column == step + 1, first, 0.0), axis=1, keepdims=True)
    end = jnp.where(step[:, :1] == steps - 1, float(seq_len), end)
    at = lax.broadcasted_iota(jnp.int32, (steps, seq_len), 1).astype(f32)
    inside = (at >= begin) & (at < end)
    sums = jnp.sum(jnp.where(inside, reward, 0.0), axis=1, keepdims=True)
    sums_ref[...] = jnp.broadcast_to(sums, sums_ref.shape)
    total = jnp.sum(beta_scale * margin, axis=1, keepdims=True)
    weight = beta_scale * (1.0 / (1.0 + jnp.exp(-total)) - label)
    row = lax.broadcasted_iota(jnp.int32, weight.shape, 0)
    position = lax.broadcasted_iota(jnp.int32, (seq_len, 1), 0).astype(f32)
    for seq, read_ref in held_rows(place_ref, own_ref, far_ref, moved_ref, across_ref):
        w = jnp.sum(jnp.where(row == seq, weight, 0.0), axis=0, keepdims=True)
        live = position < jnp.sum(jnp.where(row == seq, length, 0.0), axis=0, keepdims=True)
        slope_ref[seq] = (jnp.where(live, w, 0.0) * read_ref[...].astype(f32)).astype(bf16)
    columns = columns_ref[...].reshape(groups * seq_len, share)
    slope = slope_ref[...].reshape(groups * seq_len, slope_ref.shape[2])
    grad = lax.dot_general(
        columns, slope, (((0,), (0,)), ((), ())), preferred_element_type=f32
    ).astype(bf16)
    part = grad_ref.shape[1]
    for yh in range(2):
        for yl in range(2):
            at = (2 * yl + yh) * part
            for zl in range(4):
                piece = grad[at : at + part, 128 * zl : 128 * (zl + 1)]
                grad_ref[4 * zl + 2 * yh + yl] = piece


def grad_call(place, bounds, small, columns, reads):
    groups, seq_len, share = columns.shape
    features = reads[0].shape[1]
    return pl.pallas_call(
        grad_kernel,
        in_specs=[SMEM] + [VMEM] * 7,
        out_specs=[VMEM, VMEM],
        out_shape=[
            jax.ShapeDtypeStruct((16, share // 4, features // 4), bf16),
            jax.ShapeDtypeStruct((bounds.shape[1], seq_len), f32),
        ],
        scratch_shapes=[pltpu.VMEM((groups, seq_len, features), bf16)],
        compiler_params=pltpu.CompilerParams(vmem_limit_bytes=VMEM_LIMIT),
    )(place, bounds, small, columns, *reads)


def shifted(block, axes):
    pairs = [[(i, (i - shift) % 4) for i in range(4)] for shift in OFFSETS[1:]]
    return [block] + [lax.ppermute(block, axes, pair) for pair in pairs]


def on_device(
    hidden, norm_gain, quant_ref, scale_ref, weight_prm, readout, lengths, bounds, labels
):
    seq_len, width = hidden.shape[1:]
    features = readout.shape[2]
    head_size = features // scale_ref.shape[0]
    group = lax.axis_size(GROUP)
    x, y_lo, core = lax.axis_index("x"), lax.axis_index("yl"), lax.axis_index("c")
    place = jnp.stack([x, y_lo, core]).astype(jnp.int32)
    swap = [(0, 1), (1, 0)]
    pieces = norm_call(hidden[0], norm_gain[None], group)
    columns = exchange(pieces, GROUP)
    weight_prm, _ = lax.optimization_barrier((weight_prm, pieces))
    expanded = jnp.repeat(scale_ref.T, head_size, axis=1)
    ref_local = (quant_ref.astype(f32) * expanded).astype(bf16)
    delta = (weight_prm.astype(f32) - ref_local.astype(f32)).astype(bf16)
    delta_other = lax.ppermute(delta, "yl", swap)
    own, _, _ = lax.optimization_barrier((readout[0], pieces, delta))
    pair = [jnp.where(y_lo == k, delta, delta_other) for k in range(2)]
    delta = jnp.concatenate(pair, axis=0)
    near = shifted(own, ("x",))
    late, _ = lax.optimization_barrier((own, delta))
    far_own = lax.ppermute(late, "c", swap)
    tags = jnp.concatenate([labels, lengths])
    across = lax.all_gather(near[3], "c")
    moved = jnp.stack(near[1:3])
    moved, across, delta, far_own, place, tags = lax.optimization_barrier(
        (moved, across, delta, far_own, place, tags)
    )
    reads = [own, far_own, lax.all_gather(moved, "c"), across]
    small = exchange(margin_call(place, tags, delta, columns, reads), GROUP)
    grad, sums = grad_call(place, bounds, small, columns, reads)
    grad = wide_sum(exchange(grad, ("zl", "yh", "yl"))).astype(bf16)
    grad = wide_sum(lax.all_gather(grad, "zh")).astype(bf16)
    grad = spread(grad, ("yh", "zl"))
    grad, step_rewards = place_call(sums, grad, lax.axis_size("yh"))
    return step_rewards, grad


def solution(mesh):
    fine = Mesh(mesh.devices.reshape(2, 4, 4, 2, 4, 2), AXES)
    every = REP + FSDP
    in_specs = (
        P(every, None, None),
        P(),
        P(FSDP, None),
        P(None, FSDP),
        P(FSDP, None),
        P(every, None, None),
        P(every),
        P(every, None),
        P(every),
    )
    out_specs = (P(every, None), P(FSDP, None))
    return jax.shard_map(
        on_device, mesh=fine, in_specs=in_specs, out_specs=out_specs, check_vma=False
    )
```
